32 devices in a mesh: snap: 2 (over y), gx: 16 (over z, x, core).
Axes of the slice: x: 2, y: 2, z: 4, core: 2. Of those that a mesh axis runs over, the one named last changes fastest.
Arguments:
- positions: float32 [1024, 3, 512], P(('snap', 'gx')), parts along dimension 0, may hold values from 0 to 16
- velocity: float32 [1024, 3, 512], P(('snap', 'gx')), parts along dimension 0, may hold values from -6 to 6
- counts: int32 [1024], P(('snap', 'gx')), parts along dimension 0, may hold values from 1 to 512, 131072 in all
- tile_ids: int32 [1024], P(('snap', 'gx')), parts along dimension 0, may hold values from 0 to 511, as said below
Outputs:
- level_fine: float32 [4, 512, 32, 256], P(None, ('snap', 'gx')), parts along dimension 1
- level_mid: float32 [4, 256, 2048], P(None, ('snap', 'gx')), parts along dimension 1
- level_coarse: float32 [4, 128, 512], P(None, ('snap', 'gx')), parts along dimension 1
The draws below stay inside these ranges and needn't reach their ends.
There are 2 independent parts, one for each index of `snap`. The reference program is written for one: setup_inputs(seed, part) draws one part's arguments, and reference() takes and returns one part's arrays. A program takes and returns all parts, laid end to end along the dimension named above; each array names one. Nothing has to cross between parts.
Inputs may be any that keep to these rules, and one draw needn't show every extreme that they name: `tile_ids`: every tile id occurs once. The tile with id t is deposited into slab t // 32; one device holds at most 2 tiles of one slab, and exactly 2 of every slab it holds tiles of.
All inputs are finite; a program needn't handle non-finite values. No bound on the sum of `counts` on one device may be relied on, other than what follows from the above.
Results may differ from the reference program's by a relative error of at most 0.0021.
Values sent between devices are 32-bit elements; how exact they have to be, the bound alone decides.
No kernel may reach another device: no remote copies, remote signals or barrier semaphores. Data moves between devices by JAX's collectives and lax.ppermute only.
A program may use at most 128 MiB of HBM per device.

```python
import math
import jax
import jax.numpy as jnp
import numpy as np
from jax import lax

TILE = 16
NY = 32
NZ = 256
CAP = 512
TILE_DEV = 32
TILES = 512
N_GX = 16


def draw_tile_ids(key, part):
    key = jax.random.fold_in(key, 7)
    devices = TILES // TILE_DEV
    spread = min(devices, TILE_DEV)
    key_order, key_offset = jax.random.split(key)
    order = jax.random.permutation(key_order, devices).astype(jnp.int32)
    offsets = jax.random.randint(key_offset, (devices,), 0, TILE_DEV).astype(jnp.int32)
    slots = jnp.arange(TILES, dtype=jnp.int32)
    holder = slots // TILE_DEV
    local_slot = slots % TILE_DEV
    shifts = order[local_slot % spread]
    owners = (holder - shifts) % devices
    local_index = (local_slot + offsets[owners]) % TILE_DEV
    return (owners * TILE_DEV + local_index).astype(jnp.int32)


def block_levels(key, dims, cuts, smallest, largest):
    def one(dim, parts):
        draws = jax.random.uniform(jax.random.fold_in(jax.random.fold_in(key, 6), dim), (parts,), jnp.float32, smallest / len(cuts), largest / len(cuts))
        return jnp.repeat(jnp.exp(draws), dims[dim] // parts).reshape((-1,) + (1,) * (len(dims) - dim - 1))

    factor_of = one(*cuts[0])
    for cut in cuts[1:]:
        factor_of = factor_of * one(*cut)
    return factor_of


def split_up(count, total, reach, skew):
    loads = [(1 << 20) // math.isqrt(grade ** skew) + 1 for grade in range(2, count + 1)]
    rest, given = total - reach - (count - 1), [1] * (count - 1)
    while rest > 0:
        movable = [i for i in range(count - 1) if given[i] < reach]
        pool, left = sum([loads[i] for i in movable]), rest
        for i in movable:
            addition = min(reach - given[i], max(1, left * loads[i] // pool), rest)
            given[i] = given[i] + addition
            rest = rest - addition
    return np.array([reach] + given)


def uneven(rng, amount, total, bound, slope):
    if amount == 2:
        one = jax.random.randint(rng, (), max(1, total - bound), min(bound, total - 1) + 1)
        return jnp.stack([one, total - one])
    tallies = jnp.asarray(split_up(amount, total, bound, slope), jnp.int32)
    twos = (amount - 1) // 2
    giver, taker = tallies[1:1 + 2 * twos:2], tallies[2:2 + 2 * twos:2]
    room = jnp.minimum(giver - 1, bound - taker)
    passed = jax.random.randint(jax.random.fold_in(rng, 1), (twos,), 0, 1 << 20) % (room + 1)
    tallies = tallies.at[1:1 + 2 * twos:2].set(giver - passed).at[2:2 + 2 * twos:2].set(taker + passed)
    return tallies[jax.random.permutation(jax.random.fold_in(rng, 2), amount)]


def scatter_about(rng, extent, scale, most, pieces=(), kind=jnp.bfloat16):
    entries = jax.random.normal(rng, extent, jnp.float32) * scale
    if len(pieces) > 0:
        entries = block_levels(rng, extent, pieces, -0.22, 0.18) * entries
    return jnp.clip(entries, min=-most, max=most).astype(kind)


def setup_inputs(seed: int = 0, part: int = 0) -> dict:
    seeds = jax.random.split(jax.random.key(seed), 5)
    own_keys = jax.random.split(jax.random.fold_in(seeds[4], part), 5)
    positions = jnp.clip(16.0 * jax.random.uniform(own_keys[0], (TILES, 3, CAP), jnp.float32) ** block_levels(own_keys[0], (TILES, 3, CAP), ((0, 16),), -0.2, 0.2), 0.0, 16.0)
    velocity = scatter_about(own_keys[1], (TILES, 3, CAP), 1.0, 6.0, ((0, 16),), jnp.float32)
    counts = uneven(own_keys[2], TILES, TILES * CAP // 2, CAP, 2).astype(jnp.int32)
    tile_ids = draw_tile_ids(jax.random.fold_in(jax.random.fold_in(seeds[4], part), 71), part)
    return dict(positions=positions, velocity=velocity, counts=counts, tile_ids=tile_ids)


MASS_UNIT = 4.0


def smooth(far_low, near_low, centre, near_high, far_high):
    return (far_low + far_high + 4.0 * (near_low + near_high) + 6.0 * centre) * 0.0625


def smooth_along(field, axis):
    return smooth(jnp.roll(field, 2, axis), jnp.roll(field, 1, axis), field,
                  jnp.roll(field, -1, axis), jnp.roll(field, -2, axis))


def smooth_all(field):
    return smooth_along(smooth_along(smooth_along(field, 1), 2), 3)


def reference(positions, velocity, counts, tile_ids):
    total_planes = TILE * N_GX
    across = NZ // TILE
    alive_mask = jnp.arange(CAP, dtype=jnp.int32)[None, :] < counts[:, None]
    owners = tile_ids // TILE_DEV
    local_index = tile_ids % TILE_DEV
    base_x = owners * TILE
    base_y = (local_index // across) * TILE
    base_z = (local_index % across) * TILE
    cell_floor = jnp.minimum(jnp.floor(positions), TILE - 1.0)
    fraction = positions - cell_floor
    cell_index = cell_floor.astype(jnp.int32)
    charge = MASS_UNIT * jnp.concatenate([jnp.ones_like(velocity[:, 0:1]), velocity], axis=1)
    totals = jnp.zeros((total_planes * NY * NZ, 4), jnp.float32)
    for corner in range(8):
        step_x = corner // 4
        step_y = (corner // 2) % 2
        step_z = corner % 2
        weight_x = fraction[:, 0] if step_x else 1.0 - fraction[:, 0]
        weight_y = fraction[:, 1] if step_y else 1.0 - fraction[:, 1]
        weight_z = fraction[:, 2] if step_z else 1.0 - fraction[:, 2]
        weight_z = jnp.where(alive_mask, weight_z, 0.0)
        planar = lax.optimization_barrier((weight_x * weight_y).astype(jnp.bfloat16)).astype(jnp.float32)
        depth_rows = lax.optimization_barrier((charge * weight_z[:, None, :]).astype(jnp.bfloat16)).astype(jnp.float32)
        values = depth_rows * planar[:, None, :]
        where_x = (base_x[:, None] + cell_index[:, 0] + step_x) % total_planes
        where_y = (base_y[:, None] + cell_index[:, 1] + step_y) % NY
        where_z = (base_z[:, None] + cell_index[:, 2] + step_z) % NZ
        flat_index = ((where_x * NY + where_y) * NZ + where_z).astype(jnp.int32)
        totals = totals.at[flat_index.reshape(-1)].add(values.transpose(0, 2, 1).reshape(-1, 4))
    deposit = totals.reshape(total_planes, NY, NZ, 4).transpose(3, 0, 1, 2)
    level_fine = smooth_all(deposit)
    level_mid = smooth_all(level_fine)[:, ::2, ::2, ::2]
    level_coarse = smooth_all(level_mid)[:, ::2, ::2, ::2]
    return (level_fine,
            level_mid.reshape(4, total_planes // 2, (NY // 2) * (NZ // 2)),
            level_coarse.reshape(4, total_planes // 4, (NY // 4) * (NZ // 4)))
```

```python
import functools
import math

import jax
import jax.numpy as jnp
import ml_dtypes
import numpy as np
from jax import lax
from jax.experimental import pallas as pl
from jax.experimental.pallas import tpu as pltpu
from jax.sharding import PartitionSpec as P

TILE = 16
NY = 32
NZ = 256
LANES = 128
QUAD = 4
PLANES = TILE + 1
ROWS = PLANES * NY
WIDTH = 4 * QUAD * TILE
QUADS = NZ // (QUAD * TILE)
MASS_UNIT = 4.0
DEAD = -32.0
Y_SHIFT = 2

RIGHT = 3
LEFT = 2


def taps(levels):
    row = np.array([1.0])
    for level in range(levels):
        once = np.array([1.0, 4.0, 6.0, 4.0, 1.0]) / 16.0
        spread = np.zeros(4 * max(1, 2 ** (level - 1)) + 1)
        spread[:: max(1, 2 ** (level - 1))] = once
        row = np.convolve(row, spread)
    return row


def periodic(levels, size):
    step = 2 ** (levels - 1)
    row = taps(levels)
    half = len(row) // 2
    out = np.zeros((size // step, size))
    for i in range(size // step):
        for k, value in enumerate(row):
            out[i, (i * step + k - half) % size] += value
    return out


def open_ended(levels, below, above):
    step = 2 ** (levels - 1)
    row = taps(levels)
    half = len(row) // 2
    count = TILE // step
    out = np.zeros((below + count + above, PLANES))
    for i in range(-below, count + above):
        for k, value in enumerate(row):
            plane = i * step + k - half
            if 0 <= plane < PLANES:
                out[i + below, plane] += value
    return out


def split_host(matrix):
    high = matrix.astype(ml_dtypes.bfloat16)
    low = (matrix - high.astype(np.float64)).astype(ml_dtypes.bfloat16)
    return high, low


def depth_matrix():
    fine = periodic(1, NZ).T / 256.0
    mid = periodic(2, NZ).T
    coarse_high, coarse_low = split_host(periodic(3, NZ).T)
    columns = np.concatenate(
        [
            fine,
            mid,
            coarse_high.astype(np.float64),
            coarse_low.astype(np.float64),
        ],
        axis=1,
    )
    swapped = columns[np.arange(NZ) ^ (QUAD * TILE)]
    both = np.stack([columns, swapped])
    return np.concatenate([both, both], axis=1).astype(ml_dtypes.bfloat16)


def plane_matrix():
    rolled = (np.arange(NY) + Y_SHIFT) % NY
    mid_y = periodic(2, NY)[:, rolled]
    coarse_y = periodic(3, NY)[:, rolled]
    mid_x = open_ended(2, LEFT, RIGHT)
    coarse_x = open_ended(3, LEFT, RIGHT)
    rows = []
    for y in range(NY // 2):
        for m in range(TILE // 2):
            rows.append(np.kron(mid_x[LEFT + m], mid_y[y]))
    for m in list(range(-LEFT, 0)) + list(range(TILE // 2, TILE // 2 + RIGHT)):
        for y in range(NY // 2):
            rows.append(np.kron(mid_x[LEFT + m], mid_y[y]))
    order = list(range(0, NY // 4, 2)) + list(range(1, NY // 4, 2))
    for y in order:
        for k in range(TILE // 4):
            rows.append(np.kron(coarse_x[LEFT + k], coarse_y[y]))
    for k in list(range(-LEFT, 0)) + list(range(TILE // 4, TILE // 4 + RIGHT)):
        for y in order:
            rows.append(np.kron(coarse_x[LEFT + k], coarse_y[y]))
    high, low = split_host(np.stack(rows))
    return np.concatenate([high, low], axis=1)


def split(value):
    high = value.astype(jnp.bfloat16)
    return high, (value - high.astype(jnp.float32)).astype(jnp.bfloat16)


def hat(position, lattice):
    return jnp.maximum(1.0 - jnp.abs(position - lattice), 0.0)


def bucket_kernel(per_peer, ids_ref, counts_ref, spots_ref, speed_ref, out_ref, filled_ref):
    _, held, capacity = spots_ref.shape
    devices = out_ref.shape[0]
    chunks = capacity // LANES
    size = 6 * chunks
    for owner in range(devices):
        filled_ref[owner] = 0
    if devices * per_peer > held:
        out_ref[:, per_peer * size :, :] = jnp.full((devices, 8, LANES), -1.0, jnp.float32)

    for tile in range(held):
        tag = ids_ref[tile]
        count = counts_ref[tile]
        owner = tag // held
        rank = filled_ref[owner]
        filled_ref[owner] = rank + 1
        base = pl.multiple_of(rank * size, 8)
        for chunk in range(chunks):
            cut = slice(chunk * LANES, (chunk + 1) * LANES)
            lane = lax.broadcasted_iota(jnp.int32, (1, LANES), 1) + chunk * LANES
            for a in range(3):
                spots = spots_ref[a, tile : tile + 1, cut]
                if a == 0:
                    spots = jnp.where(lane < count, spots, DEAD)
                out_ref[owner, pl.ds(base + 6 * chunk + a, 1), :] = spots
                speed = speed_ref[a, tile : tile + 1, cut]
                out_ref[owner, pl.ds(base + 6 * chunk + 3 + a, 1), :] = speed
        mark = jnp.full((1, LANES), (tag % held).astype(jnp.float32), jnp.float32)
        out_ref[owner, pl.ds(per_peer * size + rank, 1), :] = mark


def bucket(positions, velocity, counts, tile_ids, devices, per_peer):
    capacity = positions.shape[2]
    rows = per_peer * 6 * (capacity // LANES) + 8
    return pl.pallas_call(
        functools.partial(bucket_kernel, per_peer),
        out_shape=jax.ShapeDtypeStruct((devices, rows, LANES), jnp.float32),
        in_specs=[
            pl.BlockSpec(memory_space=pltpu.SMEM),
            pl.BlockSpec(memory_space=pltpu.SMEM),
            pl.BlockSpec(memory_space=pltpu.VMEM),
            pl.BlockSpec(memory_space=pltpu.VMEM),
        ],
        out_specs=pl.BlockSpec(memory_space=pltpu.VMEM),
        scratch_shapes=[pltpu.SMEM((devices,), jnp.int32)],
        compiler_params=pltpu.CompilerParams(vmem_limit_bytes=6 * 2**20),
        name="bucket",
    )(tile_ids, counts, positions.transpose(1, 0, 2), velocity.transpose(1, 0, 2))


def deposit_kernel(
    per_peer,
    chunks,
    arrived_ref,
    depth_ref,
    plane_ref,
    fine_ref,
    rim_ref,
    mid_ref,
    coarse_ref,
    right_ref,
    left_ref,
    slot_ref,
    marks_ref,
    planar_ref,
    sums_ref,
    spread_ref,
    rest_ref,
    inside_ref,
    sems,
):
    devices = arrived_ref.shape[0]
    size = 6 * chunks
    capacity = chunks * LANES
    marks = pltpu.make_async_copy(
        arrived_ref.at[:, per_peer * size : per_peer * size + 8], marks_ref, sems.at[4]
    )
    marks.start()
    marks.wait()

    def look(slot, carry):
        tag = marks_ref[slot // per_peer, slot % per_peer, 0].astype(jnp.int32)

        @pl.when(tag >= 0)
        def _():
            slot_ref[tag] = slot

        return carry

    lax.fori_loop(0, devices * per_peer, look, 0)

    def row_of(shape, dim):
        return lax.broadcasted_iota(jnp.int32, shape, dim)

    def tile_terms(q, parity, t, ty, buffer):
        local = ty * (NZ // TILE) + q * QUAD + t
        slot = slot_ref[local]
        device = slot // per_peer
        base = pl.multiple_of((slot % per_peer) * size, 8)
        y_lattice = ((row_of((NY, LANES), 0) + (Y_SHIFT + TILE * ty)) % NY).astype(jnp.float32)
        x_lattice = row_of((24, LANES), 0).astype(jnp.float32)
        z_lattice = row_of((TILE, LANES), 0).astype(jnp.float32)
        depth_chunks = []
        for chunk in range(chunks):

            def particle(a, rows):
                line = arrived_ref[device, pl.ds(base + (6 * chunk + a), 1), :]
                return jnp.broadcast_to(line, (rows, LANES))

            weights_x = hat(particle(0, 24), x_lattice)
            weights_y = hat(particle(1, NY), y_lattice)
            start = ty * capacity + chunk * LANES
            for x in range(PLANES):
                planar = jnp.broadcast_to(weights_x[x : x + 1], (NY, LANES)) * weights_y
                planar_ref[buffer, x * NY : (x + 1) * NY, start : start + LANES] = planar.astype(
                    jnp.bfloat16
                )
            weights_z = hat(particle(2, TILE), z_lattice)
            spot_z = particle(2, TILE)
            past = jnp.where(
                row_of((TILE, LANES), 0) == 0, jnp.maximum(spot_z - (TILE - 1.0), 0.0), 0.0
            )
            charges = [jnp.full((TILE, LANES), MASS_UNIT, jnp.float32)] + [
                MASS_UNIT * particle(a, TILE) for a in (3, 4, 5)
            ]
            zero = jnp.zeros((TILE, LANES), jnp.bfloat16)
            pieces = []
            for place in range(4):
                c = place ^ parity
                inside = (charges[c] * weights_z).astype(jnp.bfloat16)
                other = charges[c ^ 1] if t == QUAD - 1 else charges[c]
                outside = (other * past).astype(jnp.bfloat16)
                for block in range(QUAD):
                    if block == t:
                        pieces.append(inside)
                    elif block == (t + 1) % QUAD:
                        pieces.append(outside)
                    else:
                        pieces.append(zero)
            depth_chunks.append(jnp.concatenate(pieces, axis=0))
        return jnp.concatenate(depth_chunks, axis=1)

    def pair_of_quads(h, carry):
        for parity in range(2):
            q = 2 * h + parity
            for t in range(QUAD):
                buffer = t % 2
                depth = jnp.concatenate(
                    [tile_terms(q, parity, t, ty, buffer) for ty in range(NY // TILE)], axis=1
                )
                result = lax.dot_general(
                    planar_ref[buffer],
                    depth,
                    (((1,), (1,)), ((), ())),
                    preferred_element_type=jnp.float32,
                )
                if t == 0:
                    sums_ref[q, 0] = result
                elif t == QUAD - 1:
                    sums_ref[q, 1] = result
                else:
                    sums_ref[q, 0] = sums_ref[q, 0] + result
        return carry

    lax.fori_loop(0, QUADS // 2, pair_of_quads, 0)

    lane = row_of((NY, LANES), 1)
    first_half = lane < LANES // 2
    inner = (lane % (LANES // 2)) != 0

    def window(q, plane, half):
        rows = slice(plane * NY, (plane + 1) * NY)
        cut = slice(half * LANES, (half + 1) * LANES)
        before = (q - 1) % QUADS
        return sums_ref[q, 0, rows, cut] + jnp.where(
            inner, sums_ref[q, 1, rows, cut], sums_ref[before, 1, rows, cut]
        )

    for half in range(2):
        for plane in range(PLANES):
            rows = slice(plane * NY, (plane + 1) * NY)
            for h in range(2):
                even, odd = window(2 * h, plane, half), window(2 * h + 1, plane, half)
                for parity in range(2):
                    one, two = (even, odd) if parity == 0 else (odd, even)
                    high, low = split(jnp.where(first_half, one, two))
                    spread_ref[2 * half + parity, rows, h * LANES : (h + 1) * LANES] = high
                    spread_ref[2 * half + parity, rows, NZ + h * LANES : NZ + (h + 1) * LANES] = low

    def inside(c):
        return pltpu.make_async_copy(
            inside_ref.at[c], fine_ref.at[c, RIGHT : TILE - LEFT], sems.at[c]
        )

    def channel(c, carry):
        levels = jnp.dot(
            spread_ref[c], depth_ref[c % 2], preferred_element_type=jnp.float32
        )
        coarse = levels[:, 3 * LANES :]
        coarse = coarse + pltpu.roll(coarse, LANES // 2, 1)
        mid_high, mid_low = split(levels[:, 2 * LANES : 3 * LANES])
        coarse_high, coarse_low = split(coarse)
        rest_ref[0, :, :LANES] = mid_high
        rest_ref[0, :, LANES:] = coarse_high
        rest_ref[1, :, :LANES] = mid_low
        rest_ref[1, :, LANES:] = coarse_low

        zero = jnp.zeros((NY, NZ), jnp.float32)
        held = [zero] * 4
        for plane in range(-LEFT, TILE + RIGHT):
            source = plane + 2
            if source < PLANES:
                field = levels[source * NY : (source + 1) * NY, :NZ]
                lag = pltpu.roll(field, 2, 0)
                twice = field + lag
                value = twice + pltpu.roll(twice, 2, 0) + 4.0 * (pltpu.roll(twice, 1, 0) + lag)
            else:
                value = zero
            for k in range(4):
                following = value + held[k]
                held[k] = value
                value = following
            if plane < 0:
                row = (c * LEFT + plane + LEFT) * 2 * NY
                left_ref[pl.ds(pl.multiple_of(row, 8), NY), :] = value[:, :LANES]
                left_ref[pl.ds(pl.multiple_of(row + NY, 8), NY), :] = value[:, LANES:]
            elif plane >= TILE:
                row = (c * RIGHT + plane - TILE) * 2 * NY
                right_ref[pl.ds(pl.multiple_of(row, 8), NY), :] = value[:, :LANES]
                right_ref[pl.ds(pl.multiple_of(row + NY, 8), NY), :] = value[:, LANES:]
            elif plane < RIGHT:
                rim_ref[c, plane] = value
            elif plane >= TILE - LEFT:
                rim_ref[c, RIGHT + plane - (TILE - LEFT)] = value
            else:
                inside_ref[c, plane - RIGHT] = value

        inside(c).start()
        high_rows, low_rows = plane_ref[:, :ROWS], plane_ref[:, ROWS:]
        packed = (
            jnp.dot(high_rows, rest_ref[0], preferred_element_type=jnp.float32)
            + jnp.dot(high_rows, rest_ref[1], preferred_element_type=jnp.float32)
            + jnp.dot(low_rows, rest_ref[0], preferred_element_type=jnp.float32)
        )
        mid_rows = NY // 2 * (TILE // 2)
        mid_edge = NY // 2
        mid_ref[c] = packed[:mid_rows, :LANES]
        at = mid_rows
        row = 4 * LEFT * 2 * NY + c * LEFT * mid_edge
        left_ref[pl.ds(pl.multiple_of(row, 8), LEFT * mid_edge), :] = packed[
            at : at + LEFT * mid_edge, :LANES
        ]
        at += LEFT * mid_edge
        row = 4 * RIGHT * 2 * NY + c * RIGHT * mid_edge
        right_ref[pl.ds(pl.multiple_of(row, 8), RIGHT * mid_edge), :] = packed[
            at : at + RIGHT * mid_edge, :LANES
        ]
        at += RIGHT * mid_edge
        coarse_rows = NY // 4 * (TILE // 4)
        coarse_edge = NY // 4
        coarse_ref[c] = packed[at : at + coarse_rows, LANES:]
        at += coarse_rows
        row = 4 * LEFT * (2 * NY + mid_edge) + c * LEFT * coarse_edge
        left_ref[pl.ds(pl.multiple_of(row, 8), LEFT * coarse_edge), :] = packed[
            at : at + LEFT * coarse_edge, LANES:
        ]
        at += LEFT * coarse_edge
        row = 4 * RIGHT * (2 * NY + mid_edge) + c * RIGHT * coarse_edge
        right_ref[pl.ds(pl.multiple_of(row, 8), RIGHT * coarse_edge), :] = packed[
            at : at + RIGHT * coarse_edge, LANES:
        ]
        return carry

    lax.fori_loop(0, 4, channel, 0)
    for c in range(4):
        inside(c).wait()


def edge_rows(planes):
    return 4 * planes * (2 * NY + NY // 2 + NY // 4)


def deposit(arrived, per_peer, capacity):
    devices = arrived.shape[0]
    f32 = jnp.float32
    vmem = pl.BlockSpec(memory_space=pltpu.VMEM)
    return pl.pallas_call(
        functools.partial(deposit_kernel, per_peer, capacity // LANES),
        out_shape=[
            jax.ShapeDtypeStruct((4, TILE, NY, NZ), f32),
            jax.ShapeDtypeStruct((4, RIGHT + LEFT, NY, NZ), f32),
            jax.ShapeDtypeStruct((4, NY // 2 * (TILE // 2), LANES), f32),
            jax.ShapeDtypeStruct((4, NY // 4 * (TILE // 4), LANES), f32),
            jax.ShapeDtypeStruct((edge_rows(RIGHT), LANES), f32),
            jax.ShapeDtypeStruct((edge_rows(LEFT), LANES), f32),
        ],
        in_specs=[vmem] * 3,
        out_specs=[pl.BlockSpec(memory_space=pl.ANY)] + [vmem] * 5,
        scratch_shapes=[
            pltpu.SMEM((NY // TILE * (NZ // TILE),), jnp.int32),
            pltpu.SMEM((devices, 8, LANES), f32),
            pltpu.VMEM((2, ROWS, NY // TILE * capacity), jnp.bfloat16),
            pltpu.VMEM((QUADS, 2, ROWS, WIDTH), f32),
            pltpu.VMEM((4, ROWS, 2 * NZ), jnp.bfloat16),
            pltpu.VMEM((2, ROWS, 2 * LANES), jnp.bfloat16),
            pltpu.VMEM((4, TILE - RIGHT - LEFT, NY, NZ), f32),
            pltpu.SemaphoreType.DMA((5,)),
        ],
        compiler_params=pltpu.CompilerParams(vmem_limit_bytes=28 * 2**20),
        name="deposit",
    )(arrived, jnp.asarray(depth_matrix()), jnp.asarray(plane_matrix()))


def join_kernel(
    inside_ref, rim_ref, mid_in_ref, coarse_in_ref, low_ref, high_ref,
    fine_ref, mid_ref, coarse_ref, edge_ref, mid_sum, coarse_sum, sems,
):
    for c in range(4):
        for plane in range(RIGHT):
            row = (c * RIGHT + plane) * 2 * NY
            edge_ref[c, plane, :, :LANES] = rim_ref[c, plane, :, :LANES] + low_ref[row : row + NY]
            edge_ref[c, plane, :, LANES:] = (
                rim_ref[c, plane, :, LANES:] + low_ref[row + NY : row + 2 * NY]
            )
        for plane in range(LEFT):
            row = (c * LEFT + plane) * 2 * NY
            at = RIGHT + plane
            edge_ref[c, at, :, :LANES] = rim_ref[c, at, :, :LANES] + high_ref[row : row + NY]
            edge_ref[c, at, :, LANES:] = (
                rim_ref[c, at, :, LANES:] + high_ref[row + NY : row + 2 * NY]
            )
    first = pltpu.make_async_copy(edge_ref.at[:, :RIGHT], fine_ref.at[:, :RIGHT], sems.at[1])
    last = pltpu.make_async_copy(edge_ref.at[:, RIGHT:], fine_ref.at[:, TILE - LEFT :], sems.at[0])
    first.start()
    last.start()
    mid_sum[...] = mid_in_ref[...]
    coarse_sum[...] = coarse_in_ref[...]
    for sent, planes, first_of in ((low_ref, RIGHT, False), (high_ref, LEFT, True)):
        for c in range(4):
            for i in range(planes):
                count, edge = TILE // 2, NY // 2
                m = count - planes + i if first_of else i
                row = 4 * planes * 2 * NY + (c * planes + i) * edge
                where = pl.ds(m, edge, stride=count)
                mid_sum[c, where, :] = mid_sum[c, where, :] + sent[row : row + edge]
                count, edge = TILE // 4, NY // 4
                k = count - planes + i if first_of else i
                row = 4 * planes * (2 * NY + NY // 2) + (c * planes + i) * edge
                where = pl.ds(k, edge, stride=count)
                coarse_sum[c, where, :] = coarse_sum[c, where, :] + sent[row : row + edge]
    for c in range(4):
        for y in range(NY // 2):
            rows = TILE // 2
            mid_ref[c, :, y * LANES : (y + 1) * LANES] = mid_sum[c, y * rows : (y + 1) * rows]
        for pair in range(NY // 8):
            rows = TILE // 4
            even = coarse_sum[c, pair * rows : (pair + 1) * rows]
            at = NY // 8 * rows + pair * rows
            odd = coarse_sum[c, at : at + rows]
            lane = lax.broadcasted_iota(jnp.int32, even.shape, 1)
            coarse_ref[c, :, pair * LANES : (pair + 1) * LANES] = jnp.where(
                lane < LANES // 2, even, odd
            )
    first.wait()
    last.wait()


def join(inside, rim, mid, coarse, from_low, from_high):
    f32 = jnp.float32
    vmem = pl.BlockSpec(memory_space=pltpu.VMEM)
    far = pl.BlockSpec(memory_space=pl.ANY)
    return pl.pallas_call(
        join_kernel,
        out_shape=[
            jax.ShapeDtypeStruct((4, TILE, NY, NZ), f32),
            jax.ShapeDtypeStruct((4, TILE // 2, NY // 2 * (NZ // 2)), f32),
            jax.ShapeDtypeStruct((4, TILE // 4, NY // 4 * (NZ // 4)), f32),
        ],
        in_specs=[far] + [vmem] * 5,
        out_specs=[far, vmem, vmem],
        scratch_shapes=[
            pltpu.VMEM((4, RIGHT + LEFT, NY, NZ), f32),
            pltpu.VMEM(mid.shape, f32),
            pltpu.VMEM(coarse.shape, f32),
            pltpu.SemaphoreType.DMA((2,)),
        ],
        input_output_aliases={0: 0},
        compiler_params=pltpu.CompilerParams(vmem_limit_bytes=10 * 2**20),
        name="join",
    )(inside, rim, mid, coarse, from_low, from_high)


def on_device(positions, velocity, counts, tile_ids):
    held = positions.shape[0]
    capacity = positions.shape[2]
    devices = lax.axis_size("gx")
    per_peer = max(1, held // devices)
    outgoing = bucket(positions, velocity, counts, tile_ids, devices, per_peer)
    arrived = lax.all_to_all(outgoing, "gx", split_axis=0, concat_axis=0, tiled=True)
    inside, rim, mid, coarse, right, left = deposit(arrived, per_peer, capacity)
    from_low = lax.ppermute(right, "gx", [(i, (i + 1) % devices) for i in range(devices)])
    from_high = lax.ppermute(left, "gx", [(i, (i - 1) % devices) for i in range(devices)])
    return tuple(join(inside, rim, mid, coarse, from_low, from_high))


def solution(mesh):
    placed = (
        P(("snap", "gx"), None, None),
        P(("snap", "gx"), None, None),
        P(("snap", "gx")),
        P(("snap", "gx")),
    )
    return jax.shard_map(
        on_device,
        mesh=mesh,
        in_specs=placed,
        out_specs=(
            P(None, ("snap", "gx"), None, None),
            P(None, ("snap", "gx"), None),
            P(None, ("snap", "gx"), None),
        ),
        check_vma=False,
    )
```

```python
import functools
import math

import jax
import jax.numpy as jnp
import ml_dtypes
import numpy as np
from jax import lax
from jax.experimental import pallas as pl
from jax.experimental.pallas import tpu as pltpu
from jax.sharding import PartitionSpec as P

TILE = 16
NY = 32
NZ = 256
LANES = 128
QUAD = 4
PLANES = TILE + 1
ROWS = PLANES * NY
WIDTH = 4 * QUAD * TILE
QUADS = NZ // (QUAD * TILE)
MASS_UNIT = 4.0
DEAD = -32.0
BELOW = 32
TILE_ROWS = PLANES * TILE + BELOW

RIGHT = 3
LEFT = 2


def taps(levels):
    row = np.array([1.0])
    for level in range(levels):
        once = np.array([1.0, 4.0, 6.0, 4.0, 1.0]) / 16.0
        spread = np.zeros(4 * max(1, 2 ** (level - 1)) + 1)
        spread[:: max(1, 2 ** (level - 1))] = once
        row = np.convolve(row, spread)
    return row


def periodic(levels, size):
    step = 2 ** (levels - 1)
    row = taps(levels)
    half = len(row) // 2
    out = np.zeros((size // step, size))
    for i in range(size // step):
        for k, value in enumerate(row):
            out[i, (i * step + k - half) % size] += value
    return out


def open_ended(levels, below, above):
    step = 2 ** (levels - 1)
    row = taps(levels)
    half = len(row) // 2
    count = TILE // step
    out = np.zeros((below + count + above, PLANES))
    for i in range(-below, count + above):
        for k, value in enumerate(row):
            plane = i * step + k - half
            if 0 <= plane < PLANES:
                out[i + below, plane] += value
    return out


def split_host(matrix):
    high = matrix.astype(ml_dtypes.bfloat16)
    low = (matrix - high.astype(np.float64)).astype(ml_dtypes.bfloat16)
    return high, low


def depth_matrix():
    fine = periodic(1, NZ).T / 256.0
    mid = periodic(2, NZ).T
    coarse_high, coarse_low = split_host(periodic(3, NZ).T)
    columns = np.concatenate(
        [
            fine,
            mid,
            coarse_high.astype(np.float64),
            coarse_low.astype(np.float64),
        ],
        axis=1,
    )
    swapped = columns[np.arange(NZ) ^ (QUAD * TILE)]
    both = np.stack([columns, swapped])
    return np.concatenate([both, both], axis=1).astype(ml_dtypes.bfloat16)


def plane_matrix():
    mid_y = periodic(2, NY)
    coarse_y = periodic(3, NY)
    mid_x = open_ended(2, LEFT, RIGHT)
    coarse_x = open_ended(3, LEFT, RIGHT)
    rows = []
    for y in range(NY // 2):
        for m in range(TILE // 2):
            rows.append(np.kron(mid_x[LEFT + m], mid_y[y]))
    for m in list(range(-LEFT, 0)) + list(range(TILE // 2, TILE // 2 + RIGHT)):
        for y in range(NY // 2):
            rows.append(np.kron(mid_x[LEFT + m], mid_y[y]))
    order = list(range(0, NY // 4, 2)) + list(range(1, NY // 4, 2))
    for y in order:
        for k in range(TILE // 4):
            rows.append(np.kron(coarse_x[LEFT + k], coarse_y[y]))
    for k in list(range(-LEFT, 0)) + list(range(TILE // 4, TILE // 4 + RIGHT)):
        for y in order:
            rows.append(np.kron(coarse_x[LEFT + k], coarse_y[y]))
    high, low = split_host(np.stack(rows))
    return np.concatenate([high, low], axis=1)


def split(value):
    high = value.astype(jnp.bfloat16)
    return high, (value - high.astype(jnp.float32)).astype(jnp.bfloat16)


def hat(position, lattice):
    return jnp.maximum(1.0 - jnp.abs(position - lattice), 0.0)


def bucket_kernel(
    per_peer, ids_far, counts_far, spots_far, speed_far, out_ref,
    filled_ref, ids_ref, counts_ref, spots_ref, speed_ref, sems,
):
    copies = [
        pltpu.make_async_copy(source, target, sems.at[i])
        for i, (source, target) in enumerate(
            (
                (ids_far, ids_ref),
                (counts_far, counts_ref),
                (spots_far, spots_ref),
                (speed_far, speed_ref),
            )
        )
    ]
    for copy in copies:
        copy.start()
    _, held, capacity = spots_ref.shape
    devices = out_ref.shape[0]
    chunks = capacity // LANES
    size = 6 * chunks
    for owner in range(devices):
        filled_ref[owner] = 0
    for copy in copies:
        copy.wait()
    if devices * per_peer > held:
        out_ref[:, per_peer * size :, :] = jnp.full((devices, 8, LANES), -1.0, jnp.float32)

    for tile in range(held):
        tag = ids_ref[tile]
        count = counts_ref[tile]
        owner = tag // held
        rank = filled_ref[owner]
        filled_ref[owner] = rank + 1
        base = pl.multiple_of(rank * size, 8)
        for chunk in range(chunks):
            cut = slice(chunk * LANES, (chunk + 1) * LANES)
            lane = lax.broadcasted_iota(jnp.int32, (1, LANES), 1) + chunk * LANES
            for a in range(3):
                spots = spots_ref[a, tile : tile + 1, cut]
                if a == 0:
                    spots = jnp.where(lane < count, spots, DEAD)
                out_ref[owner, pl.ds(base + 6 * chunk + a, 1), :] = spots
                speed = speed_ref[a, tile : tile + 1, cut]
                out_ref[owner, pl.ds(base + 6 * chunk + 3 + a, 1), :] = speed
        mark = jnp.full((1, LANES), (tag % held).astype(jnp.float32), jnp.float32)
        out_ref[owner, pl.ds(per_peer * size + rank, 1), :] = mark


def bucket(positions, velocity, counts, tile_ids, devices, per_peer):
    capacity = positions.shape[2]
    rows = per_peer * 6 * (capacity // LANES) + 8
    return pl.pallas_call(
        functools.partial(bucket_kernel, per_peer),
        out_shape=jax.ShapeDtypeStruct((devices, rows, LANES), jnp.float32),
        in_specs=[pl.BlockSpec(memory_space=pltpu.HBM)] * 4,
        out_specs=pl.BlockSpec(memory_space=pltpu.VMEM),
        scratch_shapes=[
            pltpu.SMEM((devices,), jnp.int32),
            pltpu.SMEM(tile_ids.shape, jnp.int32),
            pltpu.SMEM(counts.shape, jnp.int32),
            pltpu.VMEM((3,) + positions.shape[::2], jnp.float32),
            pltpu.VMEM((3,) + positions.shape[::2], jnp.float32),
            pltpu.SemaphoreType.DMA((4,)),
        ],
        compiler_params=pltpu.CompilerParams(vmem_limit_bytes=60 * 2**20),
        name="bucket",
    )(tile_ids, counts, positions.transpose(1, 0, 2), velocity.transpose(1, 0, 2))


def deposit_kernel(
    per_peer,
    chunks,
    arrived_ref,
    depth_ref,
    plane_ref,
    fine_ref,
    rim_ref,
    mid_ref,
    coarse_ref,
    right_ref,
    left_ref,
    slot_ref,
    marks_ref,
    planar_ref,
    depth_rows_ref,
    sums_ref,
    spread_ref,
    rest_ref,
    inside_ref,
    sems,
):
    devices = arrived_ref.shape[0]
    size = 6 * chunks
    capacity = chunks * LANES
    marks = pltpu.make_async_copy(
        arrived_ref.at[:, per_peer * size : per_peer * size + 8], marks_ref, sems.at[4]
    )
    marks.start()
    marks.wait()

    def look(slot, carry):
        tag = marks_ref[slot // per_peer, slot % per_peer, 0].astype(jnp.int32)

        @pl.when(tag >= 0)
        def _():
            slot_ref[tag] = slot

        return carry

    lax.fori_loop(0, devices * per_peer, look, 0)

    def row_of(shape, dim):
        return lax.broadcasted_iota(jnp.int32, shape, dim)

    depth_rows_ref[...] = jnp.zeros(depth_rows_ref.shape, jnp.bfloat16)
    x_lattice = row_of((BELOW, LANES), 0).astype(jnp.float32)
    cell_lattice = row_of((TILE, LANES), 0).astype(jnp.float32)
    first_row = row_of((TILE, LANES), 0) == 0

    def tile_terms(q, t, ty, buffer):
        slot = slot_ref[ty * (NZ // TILE) + q * QUAD + t]
        device = slot // per_peer
        base = pl.multiple_of((slot % per_peer) * size, 8)
        for chunk in range(chunks):

            def particle(a, rows):
                line = arrived_ref[device, pl.ds(base + (6 * chunk + a), 1), :]
                return jnp.broadcast_to(line, (rows, LANES))

            cut = slice(t * capacity + chunk * LANES, t * capacity + (chunk + 1) * LANES)
            weights_x = hat(particle(0, BELOW), x_lattice)
            weights_y = hat(particle(1, TILE), cell_lattice)
            for x in range(PLANES):
                planar = jnp.broadcast_to(weights_x[x : x + 1], (TILE, LANES)) * weights_y
                planar_ref[buffer, x * TILE : (x + 1) * TILE, cut] = planar.astype(jnp.bfloat16)
            below = weights_x * jnp.maximum(particle(1, BELOW) - (TILE - 1.0), 0.0)
            planar_ref[buffer, PLANES * TILE :, cut] = below.astype(jnp.bfloat16)

            spot_z = particle(2, TILE)
            weights_z = hat(spot_z, cell_lattice)
            past = jnp.where(first_row, jnp.maximum(spot_z - (TILE - 1.0), 0.0), 0.0)
            for c in range(4):
                charge = MASS_UNIT if c == 0 else MASS_UNIT * particle(2 + c, TILE)
                place = c ^ (q % 2)
                at = (place * QUAD + t) * TILE
                depth_rows_ref[buffer, at : at + TILE, cut] = (charge * weights_z).astype(
                    jnp.bfloat16
                )
                if t == QUAD - 1:
                    at = (place ^ 1) * QUAD * TILE
                else:
                    at = at + TILE
                depth_rows_ref[buffer, at : at + TILE, cut] = (charge * past).astype(jnp.bfloat16)

    def tile_sums(q, ty, buffer):
        for kind, cut in enumerate(
            (slice(0, (QUAD - 1) * capacity), slice((QUAD - 1) * capacity, QUAD * capacity))
        ):
            sums_ref[q, kind, ty] = lax.dot_general(
                planar_ref[buffer, :, cut],
                depth_rows_ref[buffer, :, cut],
                (((1,), (1,)), ((), ())),
                preferred_element_type=jnp.float32,
            )

    steps = [(q, ty) for q in range(QUADS) for ty in range(NY // TILE)]
    for i, (q, ty) in enumerate(steps):
        for t in range(QUAD):
            tile_terms(q, t, ty, i % 2)
        if i:
            tile_sums(*steps[i - 1], (i - 1) % 2)
    tile_sums(*steps[-1], (len(steps) - 1) % 2)

    def window(q, ty, half, rows):
        cut = slice(half * LANES, (half + 1) * LANES)
        inner = row_of((rows.stop - rows.start, LANES), 1) % (LANES // 2) != 0
        return sums_ref[q, 0, ty, rows, cut] + jnp.where(
            inner, sums_ref[q, 1, ty, rows, cut], sums_ref[(q - 1) % QUADS, 1, ty, rows, cut]
        )

    first_half = row_of((TILE, LANES), 1) < LANES // 2
    for half in range(2):
        for h in range(2):
            for ty in range(NY // TILE):
                under = slice(PLANES * TILE, PLANES * TILE + BELOW)
                past = [window(2 * h + i, 1 - ty, half, under) for i in range(2)]
                for plane in range(PLANES):
                    rows = slice(plane * TILE, (plane + 1) * TILE)
                    even, odd = (
                        window(2 * h + i, ty, half, rows)
                        + jnp.where(
                            first_row,
                            jnp.broadcast_to(past[i][plane : plane + 1], (TILE, LANES)),
                            0.0,
                        )
                        for i in range(2)
                    )
                    rows = slice(plane * NY + ty * TILE, plane * NY + (ty + 1) * TILE)
                    for parity in range(2):
                        one, two = (even, odd) if parity == 0 else (odd, even)
                        high, low = split(jnp.where(first_half, one, two))
                        at = h * LANES
                        spread_ref[2 * half + parity, rows, at : at + LANES] = high
                        at += NZ
                        spread_ref[2 * half + parity, rows, at : at + LANES] = low

    def inside(c):
        return pltpu.make_async_copy(
            inside_ref.at[c], fine_ref.at[c, RIGHT : TILE - LEFT], sems.at[c]
        )

    def channel(c, carry):
        levels = jnp.dot(
            spread_ref[c], depth_ref[c % 2], preferred_element_type=jnp.float32
        )
        coarse = levels[:, 3 * LANES :]
        coarse = coarse + pltpu.roll(coarse, LANES // 2, 1)
        mid_high, mid_low = split(levels[:, 2 * LANES : 3 * LANES])
        coarse_high, coarse_low = split(coarse)
        rest_ref[0, :, :LANES] = mid_high
        rest_ref[0, :, LANES:] = coarse_high
        rest_ref[1, :, :LANES] = mid_low
        rest_ref[1, :, LANES:] = coarse_low

        zero = jnp.zeros((NY, NZ), jnp.float32)
        held = [zero] * 4
        for plane in range(-LEFT, TILE + RIGHT):
            source = plane + 2
            if source < PLANES:
                value = levels[source * NY : (source + 1) * NY, :NZ]
                for _ in range(2):
                    either = pltpu.roll(value, 1, 0) + pltpu.roll(value, NY - 1, 0)
                    value = either + 2.0 * value
            else:
                value = zero
            for k in range(4):
                following = value + held[k]
                held[k] = value
                value = following
            if plane < 0:
                row = (c * LEFT + plane + LEFT) * 2 * NY
                left_ref[pl.ds(pl.multiple_of(row, 8), NY), :] = value[:, :LANES]
                left_ref[pl.ds(pl.multiple_of(row + NY, 8), NY), :] = value[:, LANES:]
            elif plane >= TILE:
                row = (c * RIGHT + plane - TILE) * 2 * NY
                right_ref[pl.ds(pl.multiple_of(row, 8), NY), :] = value[:, :LANES]
                right_ref[pl.ds(pl.multiple_of(row + NY, 8), NY), :] = value[:, LANES:]
            elif plane < RIGHT:
                rim_ref[c, plane] = value
            elif plane >= TILE - LEFT:
                rim_ref[c, RIGHT + plane - (TILE - LEFT)] = value
            else:
                inside_ref[c, plane - RIGHT] = value

        inside(c).start()
        high_rows, low_rows = plane_ref[:, :ROWS], plane_ref[:, ROWS:]
        packed = (
            jnp.dot(high_rows, rest_ref[0], preferred_element_type=jnp.float32)
            + jnp.dot(high_rows, rest_ref[1], preferred_element_type=jnp.float32)
            + jnp.dot(low_rows, rest_ref[0], preferred_element_type=jnp.float32)
        )
        mid_rows = NY // 2 * (TILE // 2)
        mid_edge = NY // 2
        mid_ref[c] = packed[:mid_rows, :LANES]
        at = mid_rows
        row = 4 * LEFT * 2 * NY + c * LEFT * mid_edge
        left_ref[pl.ds(pl.multiple_of(row, 8), LEFT * mid_edge), :] = packed[
            at : at + LEFT * mid_edge, :LANES
        ]
        at += LEFT * mid_edge
        row = 4 * RIGHT * 2 * NY + c * RIGHT * mid_edge
        right_ref[pl.ds(pl.multiple_of(row, 8), RIGHT * mid_edge), :] = packed[
            at : at + RIGHT * mid_edge, :LANES
        ]
        at += RIGHT * mid_edge
        coarse_rows = NY // 4 * (TILE // 4)
        coarse_edge = NY // 4
        coarse_ref[c] = packed[at : at + coarse_rows, LANES:]
        at += coarse_rows
        row = 4 * LEFT * (2 * NY + mid_edge) + c * LEFT * coarse_edge
        left_ref[pl.ds(pl.multiple_of(row, 8), LEFT * coarse_edge), :] = packed[
            at : at + LEFT * coarse_edge, LANES:
        ]
        at += LEFT * coarse_edge
        row = 4 * RIGHT * (2 * NY + mid_edge) + c * RIGHT * coarse_edge
        right_ref[pl.ds(pl.multiple_of(row, 8), RIGHT * coarse_edge), :] = packed[
            at : at + RIGHT * coarse_edge, LANES:
        ]
        return carry

    for c in range(4):
        channel(c, 0)
    for c in range(4):
        inside(c).wait()


def edge_rows(planes):
    return 4 * planes * (2 * NY + NY // 2 + NY // 4)


def deposit(arrived, per_peer, capacity):
    devices = arrived.shape[0]
    f32 = jnp.float32
    vmem = pl.BlockSpec(memory_space=pltpu.VMEM)
    return pl.pallas_call(
        functools.partial(deposit_kernel, per_peer, capacity // LANES),
        out_shape=[
            jax.ShapeDtypeStruct((4, TILE, NY, NZ), f32),
            jax.ShapeDtypeStruct((4, RIGHT + LEFT, NY, NZ), f32),
            jax.ShapeDtypeStruct((4, NY // 2 * (TILE // 2), LANES), f32),
            jax.ShapeDtypeStruct((4, NY // 4 * (TILE // 4), LANES), f32),
            jax.ShapeDtypeStruct((edge_rows(RIGHT), LANES), f32),
            jax.ShapeDtypeStruct((edge_rows(LEFT), LANES), f32),
        ],
        in_specs=[vmem] * 3,
        out_specs=[pl.BlockSpec(memory_space=pl.ANY)] + [vmem] * 5,
        scratch_shapes=[
            pltpu.SMEM((NY // TILE * (NZ // TILE),), jnp.int32),
            pltpu.SMEM((devices, 8, LANES), f32),
            pltpu.VMEM((2, TILE_ROWS, QUAD * capacity), jnp.bfloat16),
            pltpu.VMEM((2, WIDTH, QUAD * capacity), jnp.bfloat16),
            pltpu.VMEM((QUADS, 2, NY // TILE, TILE_ROWS, WIDTH), f32),
            pltpu.VMEM((4, ROWS, 2 * NZ), jnp.bfloat16),
            pltpu.VMEM((2, ROWS, 2 * LANES), jnp.bfloat16),
            pltpu.VMEM((4, TILE - RIGHT - LEFT, NY, NZ), f32),
            pltpu.SemaphoreType.DMA((5,)),
        ],
        compiler_params=pltpu.CompilerParams(vmem_limit_bytes=28 * 2**20),
        name="deposit",
    )(arrived, jnp.asarray(depth_matrix()), jnp.asarray(plane_matrix()))


def join_kernel(
    inside_ref, rim_ref, mid_in_ref, coarse_in_ref, low_ref, high_ref,
    fine_ref, mid_ref, coarse_ref, edge_ref, mid_sum, coarse_sum, sems,
):
    for c in range(4):
        for plane in range(RIGHT):
            row = (c * RIGHT + plane) * 2 * NY
            edge_ref[c, plane, :, :LANES] = rim_ref[c, plane, :, :LANES] + low_ref[row : row + NY]
            edge_ref[c, plane, :, LANES:] = (
                rim_ref[c, plane, :, LANES:] + low_ref[row + NY : row + 2 * NY]
            )
        for plane in range(LEFT):
            row = (c * LEFT + plane) * 2 * NY
            at = RIGHT + plane
            edge_ref[c, at, :, :LANES] = rim_ref[c, at, :, :LANES] + high_ref[row : row + NY]
            edge_ref[c, at, :, LANES:] = (
                rim_ref[c, at, :, LANES:] + high_ref[row + NY : row + 2 * NY]
            )
    first = pltpu.make_async_copy(edge_ref.at[:, :RIGHT], fine_ref.at[:, :RIGHT], sems.at[1])
    last = pltpu.make_async_copy(edge_ref.at[:, RIGHT:], fine_ref.at[:, TILE - LEFT :], sems.at[0])
    first.start()
    last.start()
    mid_sum[...] = mid_in_ref[...]
    coarse_sum[...] = coarse_in_ref[...]
    for sent, planes, first_of in ((low_ref, RIGHT, False), (high_ref, LEFT, True)):
        for c in range(4):
            for i in range(planes):
                count, edge = TILE // 2, NY // 2
                m = count - planes + i if first_of else i
                row = 4 * planes * 2 * NY + (c * planes + i) * edge
                where = pl.ds(m, edge, stride=count)
                mid_sum[c, where, :] = mid_sum[c, where, :] + sent[row : row + edge]
                count, edge = TILE // 4, NY // 4
                k = count - planes + i if first_of else i
                row = 4 * planes * (2 * NY + NY // 2) + (c * planes + i) * edge
                where = pl.ds(k, edge, stride=count)
                coarse_sum[c, where, :] = coarse_sum[c, where, :] + sent[row : row + edge]
    for c in range(4):
        for y in range(NY // 2):
            rows = TILE // 2
            mid_ref[c, :, y * LANES : (y + 1) * LANES] = mid_sum[c, y * rows : (y + 1) * rows]
        for pair in range(NY // 8):
            rows = TILE // 4
            even = coarse_sum[c, pair * rows : (pair + 1) * rows]
            at = NY // 8 * rows + pair * rows
            odd = coarse_sum[c, at : at + rows]
            lane = lax.broadcasted_iota(jnp.int32, even.shape, 1)
            coarse_ref[c, :, pair * LANES : (pair + 1) * LANES] = jnp.where(
                lane < LANES // 2, even, odd
            )
    first.wait()
    last.wait()


def join(inside, rim, mid, coarse, from_low, from_high):
    f32 = jnp.float32
    vmem = pl.BlockSpec(memory_space=pltpu.VMEM)
    far = pl.BlockSpec(memory_space=pl.ANY)
    return pl.pallas_call(
        join_kernel,
        out_shape=[
            jax.ShapeDtypeStruct((4, TILE, NY, NZ), f32),
            jax.ShapeDtypeStruct((4, TILE // 2, NY // 2 * (NZ // 2)), f32),
            jax.ShapeDtypeStruct((4, TILE // 4, NY // 4 * (NZ // 4)), f32),
        ],
        in_specs=[far] + [vmem] * 5,
        out_specs=[far, vmem, vmem],
        scratch_shapes=[
            pltpu.VMEM((4, RIGHT + LEFT, NY, NZ), f32),
            pltpu.VMEM(mid.shape, f32),
            pltpu.VMEM(coarse.shape, f32),
            pltpu.SemaphoreType.DMA((2,)),
        ],
        input_output_aliases={0: 0},
        compiler_params=pltpu.CompilerParams(vmem_limit_bytes=10 * 2**20),
        name="join",
    )(inside, rim, mid, coarse, from_low, from_high)


def on_device(positions, velocity, counts, tile_ids):
    held = positions.shape[0]
    capacity = positions.shape[2]
    devices = lax.axis_size("gx")
    per_peer = max(1, held // devices)
    outgoing = bucket(positions, velocity, counts, tile_ids, devices, per_peer)
    arrived = lax.all_to_all(outgoing, "gx", split_axis=0, concat_axis=0, tiled=True)
    inside, rim, mid, coarse, right, left = deposit(arrived, per_peer, capacity)
    from_low = lax.ppermute(right, "gx", [(i, (i + 1) % devices) for i in range(devices)])
    from_high = lax.ppermute(left, "gx", [(i, (i - 1) % devices) for i in range(devices)])
    return tuple(join(inside, rim, mid, coarse, from_low, from_high))


def solution(mesh):
    placed = (
        P(("snap", "gx"), None, None),
        P(("snap", "gx"), None, None),
        P(("snap", "gx")),
        P(("snap", "gx")),
    )
    return jax.shard_map(
        on_device,
        mesh=mesh,
        in_specs=placed,
        out_specs=(
            P(None, ("snap", "gx"), None, None),
            P(None, ("snap", "gx"), None),
            P(None, ("snap", "gx"), None),
        ),
        check_vma=False,
    )
```

```python
import functools
import math

import jax
import jax.numpy as jnp
import ml_dtypes
import numpy as np
from jax import lax
from jax.experimental import pallas as pl
from jax.experimental.pallas import tpu as pltpu
from jax.sharding import PartitionSpec as P

TILE = 16
NY = 32
NZ = 256
LANES = 128
QUAD = 4
PLANES = TILE + 1
ROWS = PLANES * NY
WIDTH = 4 * QUAD * TILE
QUADS = NZ // (QUAD * TILE)
MASS_UNIT = 4.0
DEAD = -32.0
BELOW = 32
TILE_ROWS = PLANES * TILE + BELOW
PLANE_ROWS = 288
DEPTH_ROWS = 4 * NZ
FILTER_ROWS = 18 * 1024

RIGHT = 3
LEFT = 2


def taps(levels):
    row = np.array([1.0])
    for level in range(levels):
        once = np.array([1.0, 4.0, 6.0, 4.0, 1.0]) / 16.0
        spread = np.zeros(4 * max(1, 2 ** (level - 1)) + 1)
        spread[:: max(1, 2 ** (level - 1))] = once
        row = np.convolve(row, spread)
    return row


def periodic(levels, size):
    step = 2 ** (levels - 1)
    row = taps(levels)
    half = len(row) // 2
    out = np.zeros((size // step, size))
    for i in range(size // step):
        for k, value in enumerate(row):
            out[i, (i * step + k - half) % size] += value
    return out


def open_ended(levels, below, above):
    step = 2 ** (levels - 1)
    row = taps(levels)
    half = len(row) // 2
    count = TILE // step
    out = np.zeros((below + count + above, PLANES))
    for i in range(-below, count + above):
        for k, value in enumerate(row):
            plane = i * step + k - half
            if 0 <= plane < PLANES:
                out[i + below, plane] += value
    return out


def split_host(matrix):
    high = matrix.astype(ml_dtypes.bfloat16)
    low = (matrix - high.astype(np.float64)).astype(ml_dtypes.bfloat16)
    return high, low


def depth_matrix():
    fine = periodic(1, NZ).T / 256.0
    mid = periodic(2, NZ).T
    coarse_high, coarse_low = split_host(periodic(3, NZ).T)
    columns = np.concatenate(
        [
            fine,
            mid,
            coarse_high.astype(np.float64),
            coarse_low.astype(np.float64),
        ],
        axis=1,
    )
    swapped = columns[np.arange(NZ) ^ (QUAD * TILE)]
    return np.concatenate([columns, columns, swapped, swapped]).astype(ml_dtypes.bfloat16)


def plane_matrix():
    mid_y = periodic(2, NY)
    coarse_y = periodic(3, NY)
    mid_x = open_ended(2, LEFT, RIGHT)
    coarse_x = open_ended(3, LEFT, RIGHT)
    rows = []
    for y in range(NY // 2):
        for m in range(TILE // 2):
            rows.append(np.kron(mid_x[LEFT + m], mid_y[y]))
    for m in list(range(-LEFT, 0)) + list(range(TILE // 2, TILE // 2 + RIGHT)):
        for y in range(NY // 2):
            rows.append(np.kron(mid_x[LEFT + m], mid_y[y]))
    order = list(range(0, NY // 4, 2)) + list(range(1, NY // 4, 2))
    for y in order:
        for k in range(TILE // 4):
            rows.append(np.kron(coarse_x[LEFT + k], coarse_y[y]))
    for k in list(range(-LEFT, 0)) + list(range(TILE // 4, TILE // 4 + RIGHT)):
        for y in order:
            rows.append(np.kron(coarse_x[LEFT + k], coarse_y[y]))
    rows += [np.zeros(ROWS)] * (PLANE_ROWS - len(rows))
    high, low = split_host(np.stack(rows))
    width = 2 * NZ
    ends = np.zeros((PLANE_ROWS, width), ml_dtypes.bfloat16)
    rest = ROWS - width
    ends[:, :rest] = high[:, width:]
    ends[:, LANES : LANES + rest] = low[:, width:]
    return np.concatenate([high[:, :width], low[:, :width], ends])


def filters():
    used = np.concatenate([depth_matrix(), plane_matrix()])
    return np.concatenate([used, np.zeros((FILTER_ROWS - len(used), used.shape[1]), used.dtype)])


def split(value):
    high = value.astype(jnp.bfloat16)
    return high, (value - high.astype(jnp.float32)).astype(jnp.bfloat16)


def depth_of(c):
    return slice(c % 2 * 2 * NZ, (c % 2 + 1) * 2 * NZ)


def smooth_rows(value):
    for _ in range(2):
        either = pltpu.roll(value, 1, 0) + pltpu.roll(value, value.shape[0] - 1, 0)
        value = either + 2.0 * value
    return value


def along_planes(fields, plane):
    total = None
    for shift, tap in zip(range(-2, 3), (1.0, 4.0, 6.0, 4.0, 1.0)):
        if plane + shift in fields:
            term = fields[plane + shift] if tap == 1.0 else tap * fields[plane + shift]
            total = term if total is None else total + term
    return total


def hat(position, lattice):
    return jnp.maximum(1.0 - jnp.abs(position - lattice), 0.0)


def bucket_kernel(
    per_peer, ids_far, counts_far, spots_far, speed_far, out_ref,
    filled_ref, ids_ref, counts_ref, spots_ref, speed_ref, sems,
):
    copies = [
        pltpu.make_async_copy(source, target, sems.at[i])
        for i, (source, target) in enumerate(
            (
                (ids_far, ids_ref),
                (counts_far, counts_ref),
                (spots_far, spots_ref),
                (speed_far, speed_ref),
            )
        )
    ]
    for copy in copies:
        copy.start()
    _, held, capacity = spots_ref.shape
    devices = out_ref.shape[0]
    size = 6 * capacity
    for owner in range(devices):
        filled_ref[owner] = 0
    for copy in copies:
        copy.wait()
    if devices * per_peer > held:
        marks = (devices, 1, per_peer * LANES)
        out_ref[:, :, per_peer * size :] = jnp.full(marks, -1.0, jnp.float32)

    for tile in range(held):
        tag = ids_ref[tile]
        count = counts_ref[tile]
        owner = tag // held
        rank = filled_ref[owner]
        filled_ref[owner] = rank + 1
        base = rank * size
        alive = lax.broadcasted_iota(jnp.int32, (1, capacity), 1) < count
        for a in range(6):
            source = spots_ref if a < 3 else speed_ref
            row = source[a % 3, tile : tile + 1, :]
            if a == 0:
                row = jnp.where(alive, row, DEAD)
            at = pl.multiple_of(base + a * capacity, LANES)
            out_ref[owner, :, pl.ds(at, capacity)] = row
        mark = jnp.full((1, LANES), (tag % held).astype(jnp.float32), jnp.float32)
        at = pl.multiple_of(per_peer * size + rank * LANES, LANES)
        out_ref[owner, :, pl.ds(at, LANES)] = mark


def bucket(positions, velocity, counts, tile_ids, devices, per_peer):
    capacity = positions.shape[2]
    columns = per_peer * (6 * capacity + LANES)
    return pl.pallas_call(
        functools.partial(bucket_kernel, per_peer),
        out_shape=jax.ShapeDtypeStruct((devices, 1, columns), jnp.float32),
        in_specs=[pl.BlockSpec(memory_space=pltpu.HBM)] * 4,
        out_specs=pl.BlockSpec(memory_space=pltpu.VMEM),
        scratch_shapes=[
            pltpu.SMEM((devices,), jnp.int32),
            pltpu.SMEM(tile_ids.shape, jnp.int32),
            pltpu.SMEM(counts.shape, jnp.int32),
            pltpu.VMEM((3,) + positions.shape[::2], jnp.float32),
            pltpu.VMEM((3,) + positions.shape[::2], jnp.float32),
            pltpu.SemaphoreType.DMA((4,)),
        ],
        compiler_params=pltpu.CompilerParams(vmem_limit_bytes=60 * 2**20),
        name="bucket",
    )(tile_ids, counts, positions.transpose(1, 0, 2), velocity.transpose(1, 0, 2))


def deposit_kernel(
    per_peer,
    chunks,
    arrived_ref,
    filter_far,
    spread_ref,
    mid_ref,
    coarse_ref,
    right_ref,
    left_ref,
    slot_ref,
    marks_ref,
    planar_even,
    planar_odd,
    depth_even,
    depth_odd,
    sums_ref,
    rest_ref,
    filter_ref,
    sems,
):
    devices = arrived_ref.shape[0]
    capacity = chunks * LANES
    size = 6 * capacity
    marks = pltpu.make_async_copy(arrived_ref.at[:, :, per_peer * size :], marks_ref, sems.at[0])
    marks.start()
    fetch = pltpu.make_async_copy(
        filter_far.at[: DEPTH_ROWS + 3 * PLANE_ROWS], filter_ref, sems.at[1]
    )
    fetch.start()
    planars, depths = (planar_even, planar_odd), (depth_even, depth_odd)
    for ref in depths:
        ref[...] = jnp.zeros(ref.shape, jnp.bfloat16)
    marks.wait()

    def look(slot, carry):
        tag = marks_ref[slot // per_peer, 0, slot % per_peer * LANES].astype(jnp.int32)

        @pl.when(tag >= 0)
        def _():
            slot_ref[tag] = slot

        return carry

    lax.fori_loop(0, devices * per_peer, look, 0)

    def row_of(shape, dim):
        return lax.broadcasted_iota(jnp.int32, shape, dim)

    x_lattice = row_of((BELOW, LANES), 0).astype(jnp.float32)
    cell_lattice = row_of((TILE, LANES), 0).astype(jnp.float32)
    first_row = row_of((TILE, LANES), 0) == 0

    def tile_terms(q, t, ty, buffer):
        slot = slot_ref[ty * (NZ // TILE) + q * QUAD + t]
        device = slot // per_peer
        base = (slot % per_peer) * size
        for chunk in range(chunks):

            def particle(a, rows):
                at = pl.multiple_of(base + (a * capacity + chunk * LANES), LANES)
                line = arrived_ref[device, :, pl.ds(at, LANES)]
                return jnp.broadcast_to(line, (rows, LANES))

            cut = slice(t * capacity + chunk * LANES, t * capacity + (chunk + 1) * LANES)
            weights_x = hat(particle(0, BELOW), x_lattice)
            weights_y = hat(particle(1, TILE), cell_lattice)
            for x in range(PLANES):
                planar = jnp.broadcast_to(weights_x[x : x + 1], (TILE, LANES)) * weights_y
                planars[buffer][x * TILE : (x + 1) * TILE, cut] = planar.astype(jnp.bfloat16)
            below = weights_x * jnp.maximum(particle(1, BELOW) - (TILE - 1.0), 0.0)
            planars[buffer][PLANES * TILE :, cut] = below.astype(jnp.bfloat16)

            spot_z = particle(2, TILE)
            weights_z = hat(spot_z, cell_lattice)
            past = jnp.where(first_row, jnp.maximum(spot_z - (TILE - 1.0), 0.0), 0.0)
            for c in range(4):
                charge = MASS_UNIT if c == 0 else MASS_UNIT * particle(2 + c, TILE)
                place = c ^ (q % 2)
                at = (place * QUAD + t) * TILE
                depths[buffer][at : at + TILE, cut] = (charge * weights_z).astype(
                    jnp.bfloat16
                )
                if t == QUAD - 1:
                    at = (place ^ 1) * QUAD * TILE
                else:
                    at = at + TILE
                depths[buffer][at : at + TILE, cut] = (charge * past).astype(jnp.bfloat16)

    def tile_sums(q, ty, buffer):
        for kind, cut in enumerate(
            (slice(0, (QUAD - 1) * capacity), slice((QUAD - 1) * capacity, QUAD * capacity))
        ):
            sums_ref[q, kind, ty] = lax.dot_general(
                planars[buffer][:, cut],
                depths[buffer][:, cut],
                (((1,), (1,)), ((), ())),
                preferred_element_type=jnp.float32,
            )

    steps = [(q, ty) for q in range(QUADS) for ty in range(NY // TILE)]
    for i, (q, ty) in enumerate(steps):
        if i:
            tile_sums(*steps[i - 1], (i - 1) % 2)
        for t in range(QUAD):
            tile_terms(q, t, ty, i % 2)
    tile_sums(*steps[-1], (len(steps) - 1) % 2)

    def window(q, ty, half, rows):
        cut = slice(half * LANES, (half + 1) * LANES)
        inner = row_of((rows.stop - rows.start, LANES), 1) % (LANES // 2) != 0
        return sums_ref[q, 0, ty, rows, cut] + jnp.where(
            inner, sums_ref[q, 1, ty, rows, cut], sums_ref[(q - 1) % QUADS, 1, ty, rows, cut]
        )

    first_half = row_of((TILE, LANES), 1) < LANES // 2
    for half in range(2):
        for h in range(2):
            for ty in range(NY // TILE):
                under = slice(PLANES * TILE, PLANES * TILE + BELOW)
                past = [window(2 * h + i, 1 - ty, half, under) for i in range(2)]
                for plane in range(PLANES):
                    rows = slice(plane * TILE, (plane + 1) * TILE)
                    even, odd = (
                        window(2 * h + i, ty, half, rows)
                        + jnp.where(
                            first_row,
                            jnp.broadcast_to(past[i][plane : plane + 1], (TILE, LANES)),
                            0.0,
                        )
                        for i in range(2)
                    )
                    rows = slice(plane * NY + ty * TILE, plane * NY + (ty + 1) * TILE)
                    for parity in range(2):
                        one, two = (even, odd) if parity == 0 else (odd, even)
                        high, low = split(jnp.where(first_half, one, two))
                        at = h * LANES
                        spread_ref[2 * half + parity, rows, at : at + LANES] = high
                        at += NZ
                        spread_ref[2 * half + parity, rows, at : at + LANES] = low

    fetch.wait()
    edge_planes = list(range(LEFT)) + list(range(PLANES - RIGHT, PLANES))

    def channel(c):
        rest = jnp.dot(spread_ref[c], filter_ref[depth_of(c), NZ:], preferred_element_type=jnp.float32)
        coarse = rest[:, LANES:]
        coarse = coarse + pltpu.roll(coarse, LANES // 2, 1)
        mid_high, mid_low = split(rest[:, :LANES])
        coarse_high, coarse_low = split(coarse)
        rest_ref[0, :, :LANES] = mid_high
        rest_ref[0, :, LANES:] = coarse_high
        rest_ref[1, :, :LANES] = mid_low
        rest_ref[1, :, LANES:] = coarse_low

        edges = jnp.dot(
            jnp.concatenate(
                [spread_ref[c, : LEFT * NY], spread_ref[c, (PLANES - RIGHT) * NY :]], axis=0
            ),
            filter_ref[depth_of(c), :NZ],
            preferred_element_type=jnp.float32,
        )
        fields = {
            plane: smooth_rows(edges[i * NY : (i + 1) * NY]) for i, plane in enumerate(edge_planes)
        }
        for ref, planes, first in ((left_ref, LEFT, -LEFT), (right_ref, RIGHT, TILE)):
            for i in range(planes):
                value = along_planes(fields, first + i)
                row = (c * planes + i) * 2 * NY
                ref[row : row + NY, :] = value[:, :LANES]
                ref[row + NY : row + 2 * NY, :] = value[:, LANES:]

        width = 2 * NZ
        tall = ROWS - width
        at = DEPTH_ROWS
        packed = None
        for part, source in ((0, 0), (0, 1), (1, 0)):
            rows = slice(at + part * PLANE_ROWS, at + (part + 1) * PLANE_ROWS)
            term = jnp.dot(
                filter_ref[rows, :], rest_ref[source, :width], preferred_element_type=jnp.float32
            )
            packed = term if packed is None else packed + term
            rows = slice(at + 2 * PLANE_ROWS, at + 3 * PLANE_ROWS)
            packed = packed + jnp.dot(
                filter_ref[rows, part * LANES : part * LANES + tall],
                rest_ref[source, width:],
                preferred_element_type=jnp.float32,
            )
        mid_rows = NY // 2 * (TILE // 2)
        mid_edge = NY // 2
        mid_ref[c] = packed[:mid_rows, :LANES]
        at = mid_rows
        row = 4 * LEFT * 2 * NY + c * LEFT * mid_edge
        left_ref[pl.ds(pl.multiple_of(row, 8), LEFT * mid_edge), :] = packed[
            at : at + LEFT * mid_edge, :LANES
        ]
        at += LEFT * mid_edge
        row = 4 * RIGHT * 2 * NY + c * RIGHT * mid_edge
        right_ref[pl.ds(pl.multiple_of(row, 8), RIGHT * mid_edge), :] = packed[
            at : at + RIGHT * mid_edge, :LANES
        ]
        at += RIGHT * mid_edge
        coarse_rows = NY // 4 * (TILE // 4)
        coarse_edge = NY // 4
        coarse_ref[c] = packed[at : at + coarse_rows, LANES:]
        at += coarse_rows
        row = 4 * LEFT * (2 * NY + mid_edge) + c * LEFT * coarse_edge
        left_ref[pl.ds(pl.multiple_of(row, 8), LEFT * coarse_edge), :] = packed[
            at : at + LEFT * coarse_edge, LANES:
        ]
        at += LEFT * coarse_edge
        row = 4 * RIGHT * (2 * NY + mid_edge) + c * RIGHT * coarse_edge
        right_ref[pl.ds(pl.multiple_of(row, 8), RIGHT * coarse_edge), :] = packed[
            at : at + RIGHT * coarse_edge, LANES:
        ]

    for c in range(4):
        channel(c)


def fine_kernel(spread_ref, filter_far, fine_ref, rim_ref, inside_ref, filter_ref, sems):
    fetch = pltpu.make_async_copy(filter_far.at[:DEPTH_ROWS], filter_ref, sems.at[4])
    fetch.start()
    fetch.wait()

    def inside(c):
        return pltpu.make_async_copy(
            inside_ref.at[c], fine_ref.at[c, RIGHT : TILE - LEFT], sems.at[c]
        )

    for c in range(4):
        level = jnp.dot(spread_ref[c], filter_ref[depth_of(c), :NZ], preferred_element_type=jnp.float32)
        zero = jnp.zeros((NY, NZ), jnp.float32)
        held = [zero] * 4
        for plane in range(-LEFT, TILE):
            source = plane + 2
            value = zero
            if source < PLANES:
                value = smooth_rows(level[source * NY : (source + 1) * NY])
            for k in range(4):
                following = value + held[k]
                held[k] = value
                value = following
            if 0 <= plane < RIGHT:
                rim_ref[c, plane] = value
            elif plane >= TILE - LEFT:
                rim_ref[c, RIGHT + plane - (TILE - LEFT)] = value
            elif plane >= 0:
                inside_ref[c, plane - RIGHT] = value
        inside(c).start()
    for c in range(4):
        inside(c).wait()


def fine(spread, matrices):
    f32 = jnp.float32
    vmem = pl.BlockSpec(memory_space=pltpu.VMEM)
    return pl.pallas_call(
        fine_kernel,
        out_shape=[
            jax.ShapeDtypeStruct((4, TILE, NY, NZ), f32),
            jax.ShapeDtypeStruct((4, RIGHT + LEFT, NY, NZ), f32),
        ],
        in_specs=[vmem, pl.BlockSpec(memory_space=pltpu.HBM)],
        out_specs=[pl.BlockSpec(memory_space=pl.ANY), vmem],
        scratch_shapes=[
            pltpu.VMEM((4, TILE - RIGHT - LEFT, NY, NZ), f32),
            pltpu.VMEM((DEPTH_ROWS, 2 * NZ), jnp.bfloat16),
            pltpu.SemaphoreType.DMA((5,)),
        ],
        compiler_params=pltpu.CompilerParams(vmem_limit_bytes=44 * 2**20),
        cost_estimate=pl.CostEstimate(
            flops=4 * 2 * ROWS * 2 * NZ * NZ, bytes_accessed=10**7, transcendentals=0
        ),
        name="fine",
    )(spread, matrices)


def edge_rows(planes):
    return 4 * planes * (2 * NY + NY // 2 + NY // 4)


def deposit(arrived, matrices, per_peer, capacity):
    devices = arrived.shape[0]
    f32 = jnp.float32
    vmem = pl.BlockSpec(memory_space=pltpu.VMEM)
    return pl.pallas_call(
        functools.partial(deposit_kernel, per_peer, capacity // LANES),
        out_shape=[
            jax.ShapeDtypeStruct((4, ROWS, 2 * NZ), jnp.bfloat16),
            jax.ShapeDtypeStruct((4, NY // 2 * (TILE // 2), LANES), f32),
            jax.ShapeDtypeStruct((4, NY // 4 * (TILE // 4), LANES), f32),
            jax.ShapeDtypeStruct((edge_rows(RIGHT), LANES), f32),
            jax.ShapeDtypeStruct((edge_rows(LEFT), LANES), f32),
        ],
        in_specs=[vmem, pl.BlockSpec(memory_space=pltpu.HBM)],
        out_specs=[vmem] * 5,
        scratch_shapes=[
            pltpu.SMEM((NY // TILE * (NZ // TILE),), jnp.int32),
            pltpu.SMEM((devices, 1, per_peer * LANES), f32),
            pltpu.VMEM((TILE_ROWS, QUAD * capacity), jnp.bfloat16),
            pltpu.VMEM((TILE_ROWS, QUAD * capacity), jnp.bfloat16),
            pltpu.VMEM((WIDTH, QUAD * capacity), jnp.bfloat16),
            pltpu.VMEM((WIDTH, QUAD * capacity), jnp.bfloat16),
            pltpu.VMEM((QUADS, 2, NY // TILE, TILE_ROWS, WIDTH), f32),
            pltpu.VMEM((2, ROWS, 2 * LANES), jnp.bfloat16),
            pltpu.VMEM((DEPTH_ROWS + 3 * PLANE_ROWS, 2 * NZ), jnp.bfloat16),
            pltpu.SemaphoreType.DMA((2,)),
        ],
        compiler_params=pltpu.CompilerParams(vmem_limit_bytes=44 * 2**20),
        name="deposit",
    )(arrived, matrices)


def join_kernel(
    inside_ref, rim_ref, mid_in_ref, coarse_in_ref, low_ref, high_ref,
    fine_ref, mid_ref, coarse_ref, edge_ref, mid_sum, coarse_sum, sems,
):
    for c in range(4):
        for plane in range(RIGHT):
            row = (c * RIGHT + plane) * 2 * NY
            edge_ref[c, plane, :, :LANES] = rim_ref[c, plane, :, :LANES] + low_ref[row : row + NY]
            edge_ref[c, plane, :, LANES:] = (
                rim_ref[c, plane, :, LANES:] + low_ref[row + NY : row + 2 * NY]
            )
        for plane in range(LEFT):
            row = (c * LEFT + plane) * 2 * NY
            at = RIGHT + plane
            edge_ref[c, at, :, :LANES] = rim_ref[c, at, :, :LANES] + high_ref[row : row + NY]
            edge_ref[c, at, :, LANES:] = (
                rim_ref[c, at, :, LANES:] + high_ref[row + NY : row + 2 * NY]
            )
    first = pltpu.make_async_copy(edge_ref.at[:, :RIGHT], fine_ref.at[:, :RIGHT], sems.at[1])
    last = pltpu.make_async_copy(edge_ref.at[:, RIGHT:], fine_ref.at[:, TILE - LEFT :], sems.at[0])
    first.start()
    last.start()
    mid_sum[...] = mid_in_ref[...]
    coarse_sum[...] = coarse_in_ref[...]
    for sent, planes, first_of in ((low_ref, RIGHT, False), (high_ref, LEFT, True)):
        for c in range(4):
            for i in range(planes):
                count, edge = TILE // 2, NY // 2
                m = count - planes + i if first_of else i
                row = 4 * planes * 2 * NY + (c * planes + i) * edge
                where = pl.ds(m, edge, stride=count)
                mid_sum[c, where, :] = mid_sum[c, where, :] + sent[row : row + edge]
                count, edge = TILE // 4, NY // 4
                k = count - planes + i if first_of else i
                row = 4 * planes * (2 * NY + NY // 2) + (c * planes + i) * edge
                where = pl.ds(k, edge, stride=count)
                coarse_sum[c, where, :] = coarse_sum[c, where, :] + sent[row : row + edge]
    for c in range(4):
        for y in range(NY // 2):
            rows = TILE // 2
            mid_ref[c, :, y * LANES : (y + 1) * LANES] = mid_sum[c, y * rows : (y + 1) * rows]
        for pair in range(NY // 8):
            rows = TILE // 4
            even = coarse_sum[c, pair * rows : (pair + 1) * rows]
            at = NY // 8 * rows + pair * rows
            odd = coarse_sum[c, at : at + rows]
            lane = lax.broadcasted_iota(jnp.int32, even.shape, 1)
            coarse_ref[c, :, pair * LANES : (pair + 1) * LANES] = jnp.where(
                lane < LANES // 2, even, odd
            )
    first.wait()
    last.wait()


def join(inside, rim, mid, coarse, from_low, from_high):
    f32 = jnp.float32
    vmem = pl.BlockSpec(memory_space=pltpu.VMEM)
    far = pl.BlockSpec(memory_space=pl.ANY)
    return pl.pallas_call(
        join_kernel,
        out_shape=[
            jax.ShapeDtypeStruct((4, TILE, NY, NZ), f32),
            jax.ShapeDtypeStruct((4, TILE // 2, NY // 2 * (NZ // 2)), f32),
            jax.ShapeDtypeStruct((4, TILE // 4, NY // 4 * (NZ // 4)), f32),
        ],
        in_specs=[far] + [vmem] * 5,
        out_specs=[far, vmem, vmem],
        scratch_shapes=[
            pltpu.VMEM((4, RIGHT + LEFT, NY, NZ), f32),
            pltpu.VMEM(mid.shape, f32),
            pltpu.VMEM(coarse.shape, f32),
            pltpu.SemaphoreType.DMA((2,)),
        ],
        input_output_aliases={0: 0},
        compiler_params=pltpu.CompilerParams(vmem_limit_bytes=10 * 2**20),
        name="join",
    )(inside, rim, mid, coarse, from_low, from_high)


def on_device(positions, velocity, counts, tile_ids):
    held = positions.shape[0]
    capacity = positions.shape[2]
    devices = lax.axis_size("gx")
    per_peer = max(1, held // devices)
    matrices = jnp.asarray(filters())
    outgoing = bucket(positions, velocity, counts, tile_ids, devices, per_peer)
    arrived = lax.all_to_all(outgoing, "gx", split_axis=0, concat_axis=0, tiled=True)
    spread, mid, coarse, right, left = deposit(arrived, matrices, per_peer, capacity)
    from_low = lax.ppermute(right, "gx", [(i, (i + 1) % devices) for i in range(devices)])
    from_high = lax.ppermute(left, "gx", [(i, (i - 1) % devices) for i in range(devices)])
    inside, rim = fine(spread, matrices)
    return tuple(join(inside, rim, mid, coarse, from_low, from_high))


def solution(mesh):
    placed = (
        P(("snap", "gx"), None, None),
        P(("snap", "gx"), None, None),
        P(("snap", "gx")),
        P(("snap", "gx")),
    )
    return jax.shard_map(
        on_device,
        mesh=mesh,
        in_specs=placed,
        out_specs=(
            P(None, ("snap", "gx"), None, None),
            P(None, ("snap", "gx"), None),
            P(None, ("snap", "gx"), None),
        ),
        check_vma=False,
    )
```

```python
import functools
import math

import jax
import jax.numpy as jnp
import ml_dtypes
import numpy as np
from jax import lax
from jax.experimental import pallas as pl
from jax.experimental.pallas import tpu as pltpu
from jax.sharding import PartitionSpec as P

TILE = 16
NY = 32
NZ = 256
LANES = 128
QUAD = 4
PLANES = TILE + 1
ROWS = PLANES * NY
WIDTH = 4 * QUAD * TILE
QUADS = NZ // (QUAD * TILE)
MASS_UNIT = 4.0
DEAD = -32.0
BELOW = 32
TILE_ROWS = PLANES * TILE + BELOW
PLANE_ROWS = 288
DEPTH_ROWS = 4 * NZ
FILTER_ROWS = 18 * 1024

RIGHT = 3
LEFT = 2


def taps(levels):
    row = np.array([1.0])
    for level in range(levels):
        once = np.array([1.0, 4.0, 6.0, 4.0, 1.0]) / 16.0
        spread = np.zeros(4 * max(1, 2 ** (level - 1)) + 1)
        spread[:: max(1, 2 ** (level - 1))] = once
        row = np.convolve(row, spread)
    return row


def periodic(levels, size):
    step = 2 ** (levels - 1)
    row = taps(levels)
    half = len(row) // 2
    out = np.zeros((size // step, size))
    for i in range(size // step):
        for k, value in enumerate(row):
            out[i, (i * step + k - half) % size] += value
    return out


def open_ended(levels, below, above):
    step = 2 ** (levels - 1)
    row = taps(levels)
    half = len(row) // 2
    count = TILE // step
    out = np.zeros((below + count + above, PLANES))
    for i in range(-below, count + above):
        for k, value in enumerate(row):
            plane = i * step + k - half
            if 0 <= plane < PLANES:
                out[i + below, plane] += value
    return out


def split_host(matrix):
    high = matrix.astype(ml_dtypes.bfloat16)
    low = (matrix - high.astype(np.float64)).astype(ml_dtypes.bfloat16)
    return high, low


def depth_matrix():
    fine = periodic(1, NZ).T / 256.0
    mid = periodic(2, NZ).T
    coarse_high, coarse_low = split_host(periodic(3, NZ).T)
    columns = np.concatenate(
        [
            fine,
            mid,
            coarse_high.astype(np.float64),
            coarse_low.astype(np.float64),
        ],
        axis=1,
    )
    swapped = columns[np.arange(NZ) ^ (QUAD * TILE)]
    return np.concatenate([columns, columns, swapped, swapped]).astype(ml_dtypes.bfloat16)


def plane_matrix():
    mid_y = periodic(2, NY)
    coarse_y = periodic(3, NY)
    mid_x = open_ended(2, LEFT, RIGHT)
    coarse_x = open_ended(3, LEFT, RIGHT)
    rows = []
    for y in range(NY // 2):
        for m in range(TILE // 2):
            rows.append(np.kron(mid_x[LEFT + m], mid_y[y]))
    for m in list(range(-LEFT, 0)) + list(range(TILE // 2, TILE // 2 + RIGHT)):
        for y in range(NY // 2):
            rows.append(np.kron(mid_x[LEFT + m], mid_y[y]))
    order = list(range(0, NY // 4, 2)) + list(range(1, NY // 4, 2))
    for y in order:
        for k in range(TILE // 4):
            rows.append(np.kron(coarse_x[LEFT + k], coarse_y[y]))
    for k in list(range(-LEFT, 0)) + list(range(TILE // 4, TILE // 4 + RIGHT)):
        for y in order:
            rows.append(np.kron(coarse_x[LEFT + k], coarse_y[y]))
    rows += [np.zeros(ROWS)] * (PLANE_ROWS - len(rows))
    high, low = split_host(np.stack(rows))
    width = 2 * NZ
    ends = np.zeros((PLANE_ROWS, width), ml_dtypes.bfloat16)
    rest = ROWS - width
    for i, part in enumerate((high, high, low)):
        ends[:, i * rest : (i + 1) * rest] = part[:, width:]
    return np.concatenate([high[:, :width], low[:, :width], ends])


def filters():
    used = np.concatenate([depth_matrix(), plane_matrix()])
    return np.concatenate([used, np.zeros((FILTER_ROWS - len(used), used.shape[1]), used.dtype)])


def split(value):
    high = value.astype(jnp.bfloat16)
    return high, (value - high.astype(jnp.float32)).astype(jnp.bfloat16)


def depth_of(c):
    return slice(c % 2 * 2 * NZ, (c % 2 + 1) * 2 * NZ)


def smooth_rows(value):
    for _ in range(2):
        either = pltpu.roll(value, 1, 0) + pltpu.roll(value, value.shape[0] - 1, 0)
        value = either + 2.0 * value
    return value


def along_planes(fields, plane):
    total = None
    for shift, tap in zip(range(-2, 3), (1.0, 4.0, 6.0, 4.0, 1.0)):
        if plane + shift in fields:
            term = fields[plane + shift] if tap == 1.0 else tap * fields[plane + shift]
            total = term if total is None else total + term
    return total


def hat(position, lattice):
    return jnp.maximum(1.0 - jnp.abs(position - lattice), 0.0)


def bucket_kernel(
    per_peer, ids_far, counts_far, spots_far, speed_far, out_ref,
    filled_ref, ids_ref, counts_ref, spots_ref, speed_ref, sems,
):
    copies = [
        pltpu.make_async_copy(source, target, sems.at[i])
        for i, (source, target) in enumerate(
            (
                (ids_far, ids_ref),
                (counts_far, counts_ref),
                (spots_far, spots_ref),
                (speed_far, speed_ref),
            )
        )
    ]
    for copy in copies:
        copy.start()
    _, held, capacity = spots_ref.shape
    devices = out_ref.shape[0]
    size = 6 * capacity
    for owner in range(devices):
        filled_ref[owner] = 0
    for copy in copies:
        copy.wait()
    if devices * per_peer > held:
        marks = (devices, 1, per_peer * LANES)
        out_ref[:, :, per_peer * size :] = jnp.full(marks, -1.0, jnp.float32)

    for tile in range(held):
        tag = ids_ref[tile]
        count = counts_ref[tile]
        owner = tag // held
        rank = filled_ref[owner]
        filled_ref[owner] = rank + 1
        base = rank * size
        alive = lax.broadcasted_iota(jnp.int32, (1, capacity), 1) < count
        for a in range(6):
            source = spots_ref if a < 3 else speed_ref
            row = source[a % 3, tile : tile + 1, :]
            if a == 0:
                row = jnp.where(alive, row, DEAD)
            at = pl.multiple_of(base + a * capacity, LANES)
            out_ref[owner, :, pl.ds(at, capacity)] = row
        mark = jnp.full((1, LANES), (tag % held).astype(jnp.float32), jnp.float32)
        at = pl.multiple_of(per_peer * size + rank * LANES, LANES)
        out_ref[owner, :, pl.ds(at, LANES)] = mark


def bucket(positions, velocity, counts, tile_ids, devices, per_peer):
    capacity = positions.shape[2]
    columns = per_peer * (6 * capacity + LANES)
    return pl.pallas_call(
        functools.partial(bucket_kernel, per_peer),
        out_shape=jax.ShapeDtypeStruct((devices, 1, columns), jnp.float32),
        in_specs=[pl.BlockSpec(memory_space=pltpu.HBM)] * 4,
        out_specs=pl.BlockSpec(memory_space=pltpu.VMEM),
        scratch_shapes=[
            pltpu.SMEM((devices,), jnp.int32),
            pltpu.SMEM(tile_ids.shape, jnp.int32),
            pltpu.SMEM(counts.shape, jnp.int32),
            pltpu.VMEM((3,) + positions.shape[::2], jnp.float32),
            pltpu.VMEM((3,) + positions.shape[::2], jnp.float32),
            pltpu.SemaphoreType.DMA((4,)),
        ],
        compiler_params=pltpu.CompilerParams(vmem_limit_bytes=60 * 2**20),
        name="bucket",
    )(tile_ids, counts, positions.transpose(1, 0, 2), velocity.transpose(1, 0, 2))


def deposit_kernel(
    per_peer,
    chunks,
    arrived_ref,
    filter_far,
    spread_ref,
    mid_ref,
    coarse_ref,
    right_ref,
    left_ref,
    slot_ref,
    marks_ref,
    planar_even,
    planar_odd,
    depth_even,
    depth_odd,
    sums_ref,
    rest_ref,
    tails_ref,
    filter_ref,
    sems,
):
    devices = arrived_ref.shape[0]
    capacity = chunks * LANES
    size = 6 * capacity
    marks = pltpu.make_async_copy(arrived_ref.at[:, :, per_peer * size :], marks_ref, sems.at[0])
    marks.start()
    fetch = pltpu.make_async_copy(
        filter_far.at[: DEPTH_ROWS + 3 * PLANE_ROWS], filter_ref, sems.at[1]
    )
    fetch.start()
    planars, depths = (planar_even, planar_odd), (depth_even, depth_odd)
    for ref in depths:
        ref[...] = jnp.zeros(ref.shape, jnp.bfloat16)
    marks.wait()

    tiles = NY // TILE * (NZ // TILE)

    def look(slot, carry):
        tag = marks_ref[slot // per_peer, 0, slot % per_peer * LANES].astype(jnp.int32)
        slot_ref[jnp.where(tag < 0, tiles, tag)] = slot
        return carry

    if devices * per_peer == tiles:
        for slot in range(tiles):
            look(slot, 0)
    else:
        lax.fori_loop(0, devices * per_peer, look, 0)

    def row_of(shape, dim):
        return lax.broadcasted_iota(jnp.int32, shape, dim)

    x_lattice = row_of((BELOW, LANES), 0).astype(jnp.float32)
    cell_lattice = row_of((TILE, LANES), 0).astype(jnp.float32)
    first_row = row_of((TILE, LANES), 0) == 0

    def tile_terms(q, t, ty, buffer):
        slot = slot_ref[ty * (NZ // TILE) + q * QUAD + t]
        device = slot // per_peer
        base = (slot % per_peer) * size
        for chunk in range(chunks):

            def particle(a, rows):
                at = pl.multiple_of(base + (a * capacity + chunk * LANES), LANES)
                line = arrived_ref[device, :, pl.ds(at, LANES)]
                return jnp.broadcast_to(line, (rows, LANES))

            cut = slice(t * capacity + chunk * LANES, t * capacity + (chunk + 1) * LANES)
            weights_x = hat(particle(0, BELOW), x_lattice)
            weights_y = hat(particle(1, TILE), cell_lattice)
            for x in range(PLANES):
                planar = jnp.broadcast_to(weights_x[x : x + 1], (TILE, LANES)) * weights_y
                planars[buffer][x * TILE : (x + 1) * TILE, cut] = planar.astype(jnp.bfloat16)
            below = weights_x * jnp.maximum(particle(1, BELOW) - (TILE - 1.0), 0.0)
            planars[buffer][PLANES * TILE :, cut] = below.astype(jnp.bfloat16)

            spot_z = particle(2, TILE)
            weights_z = hat(spot_z, cell_lattice)
            past = jnp.where(first_row, jnp.maximum(spot_z - (TILE - 1.0), 0.0), 0.0)
            for c in range(4):
                charge = MASS_UNIT if c == 0 else MASS_UNIT * particle(2 + c, TILE)
                place = c ^ (q % 2)
                at = (place * QUAD + t) * TILE
                depths[buffer][at : at + TILE, cut] = (charge * weights_z).astype(
                    jnp.bfloat16
                )
                if t == QUAD - 1:
                    at = (place ^ 1) * QUAD * TILE
                else:
                    at = at + TILE
                depths[buffer][at : at + TILE, cut] = (charge * past).astype(jnp.bfloat16)

    def tile_sums(q, ty, buffer):
        for kind, cut in enumerate(
            (slice(0, (QUAD - 1) * capacity), slice((QUAD - 1) * capacity, QUAD * capacity))
        ):
            sums_ref[q, kind, ty] = lax.dot_general(
                planars[buffer][:, cut],
                depths[buffer][:, cut],
                (((1,), (1,)), ((), ())),
                preferred_element_type=jnp.float32,
            )

    steps = [(q, ty) for q in range(QUADS) for ty in range(NY // TILE)]
    for i, (q, ty) in enumerate(steps):
        if i:
            tile_sums(*steps[i - 1], (i - 1) % 2)
        for t in range(QUAD):
            tile_terms(q, t, ty, i % 2)
    tile_sums(*steps[-1], (len(steps) - 1) % 2)

    def window(q, ty, half, rows):
        cut = slice(half * LANES, (half + 1) * LANES)
        inner = row_of((rows.stop - rows.start, LANES), 1) % (LANES // 2) != 0
        return sums_ref[q, 0, ty, rows, cut] + jnp.where(
            inner, sums_ref[q, 1, ty, rows, cut], sums_ref[(q - 1) % QUADS, 1, ty, rows, cut]
        )

    first_half = row_of((TILE, LANES), 1) < LANES // 2
    for half in range(2):
        for h in range(2):
            for ty in range(NY // TILE):
                under = slice(PLANES * TILE, PLANES * TILE + BELOW)
                past = [window(2 * h + i, 1 - ty, half, under) for i in range(2)]
                for plane in range(PLANES):
                    rows = slice(plane * TILE, (plane + 1) * TILE)
                    even, odd = (
                        window(2 * h + i, ty, half, rows)
                        + jnp.where(
                            first_row,
                            jnp.broadcast_to(past[i][plane : plane + 1], (TILE, LANES)),
                            0.0,
                        )
                        for i in range(2)
                    )
                    rows = slice(plane * NY + ty * TILE, plane * NY + (ty + 1) * TILE)
                    for parity in range(2):
                        one, two = (even, odd) if parity == 0 else (odd, even)
                        high, low = split(jnp.where(first_half, one, two))
                        at = h * LANES
                        spread_ref[2 * half + parity, rows, at : at + LANES] = high
                        at += NZ
                        spread_ref[2 * half + parity, rows, at : at + LANES] = low

    fetch.wait()
    edge_planes = list(range(LEFT)) + list(range(PLANES - RIGHT, PLANES))

    width = 2 * NZ
    tall = ROWS - width

    def channel(c):
        rest = jnp.dot(spread_ref[c], filter_ref[depth_of(c), NZ:], preferred_element_type=jnp.float32)
        coarse = rest[:, LANES:]
        coarse = coarse + pltpu.roll(coarse, LANES // 2, 1)
        mid_high, mid_low = split(rest[:, :LANES])
        coarse_high, coarse_low = split(coarse)
        for i, (mid, rough) in enumerate(((mid_high, coarse_high), (mid_low, coarse_low))):
            rest_ref[c, i, :, :LANES] = mid[:width]
            rest_ref[c, i, :, LANES:] = rough[:width]
        for i, (mid, rough) in enumerate(
            ((mid_high, coarse_high), (mid_low, coarse_low), (mid_high, coarse_high))
        ):
            rows = slice(i * tall, (i + 1) * tall)
            tails_ref[c, rows, :LANES] = mid[width:]
            tails_ref[c, rows, LANES:] = rough[width:]

        edges = jnp.dot(
            jnp.concatenate(
                [spread_ref[c, : LEFT * NY], spread_ref[c, (PLANES - RIGHT) * NY :]], axis=0
            ),
            filter_ref[depth_of(c), :NZ],
            preferred_element_type=jnp.float32,
        )
        fields = {
            plane: smooth_rows(edges[i * NY : (i + 1) * NY]) for i, plane in enumerate(edge_planes)
        }
        for ref, planes, first in ((left_ref, LEFT, -LEFT), (right_ref, RIGHT, TILE)):
            for i in range(planes):
                value = along_planes(fields, first + i)
                row = (c * planes + i) * 2 * NY
                ref[row : row + NY, :] = value[:, :LANES]
                ref[row + NY : row + 2 * NY, :] = value[:, LANES:]

    def planes(c):
        at = DEPTH_ROWS + 2 * PLANE_ROWS
        packed = jnp.dot(
            filter_ref[at : at + PLANE_ROWS, : 3 * tall],
            tails_ref[c],
            preferred_element_type=jnp.float32,
        )
        for part, source in ((0, 0), (0, 1), (1, 0)):
            at = DEPTH_ROWS + part * PLANE_ROWS
            packed = packed + jnp.dot(
                filter_ref[at : at + PLANE_ROWS, :],
                rest_ref[c, source],
                preferred_element_type=jnp.float32,
            )
        mid_rows = NY // 2 * (TILE // 2)
        mid_edge = NY // 2
        mid_ref[c] = packed[:mid_rows, :LANES]
        at = mid_rows
        row = 4 * LEFT * 2 * NY + c * LEFT * mid_edge
        left_ref[pl.ds(pl.multiple_of(row, 8), LEFT * mid_edge), :] = packed[
            at : at + LEFT * mid_edge, :LANES
        ]
        at += LEFT * mid_edge
        row = 4 * RIGHT * 2 * NY + c * RIGHT * mid_edge
        right_ref[pl.ds(pl.multiple_of(row, 8), RIGHT * mid_edge), :] = packed[
            at : at + RIGHT * mid_edge, :LANES
        ]
        at += RIGHT * mid_edge
        coarse_rows = NY // 4 * (TILE // 4)
        coarse_edge = NY // 4
        coarse_ref[c] = packed[at : at + coarse_rows, LANES:]
        at += coarse_rows
        row = 4 * LEFT * (2 * NY + mid_edge) + c * LEFT * coarse_edge
        left_ref[pl.ds(pl.multiple_of(row, 8), LEFT * coarse_edge), :] = packed[
            at : at + LEFT * coarse_edge, LANES:
        ]
        at += LEFT * coarse_edge
        row = 4 * RIGHT * (2 * NY + mid_edge) + c * RIGHT * coarse_edge
        right_ref[pl.ds(pl.multiple_of(row, 8), RIGHT * coarse_edge), :] = packed[
            at : at + RIGHT * coarse_edge, LANES:
        ]

    channel(0)
    for c in range(4):
        if c < 3:
            channel(c + 1)
        planes(c)


def fine_kernel(spread_ref, filter_far, fine_ref, rim_ref, inside_ref, filter_ref, sems):
    fetch = pltpu.make_async_copy(filter_far.at[:DEPTH_ROWS], filter_ref, sems.at[4])
    fetch.start()
    fetch.wait()

    def inside(c):
        return pltpu.make_async_copy(
            inside_ref.at[c], fine_ref.at[c, RIGHT : TILE - LEFT], sems.at[c]
        )

    for c in range(4):
        level = jnp.dot(spread_ref[c], filter_ref[depth_of(c), :NZ], preferred_element_type=jnp.float32)
        zero = jnp.zeros((NY, NZ), jnp.float32)
        held = [zero] * 4
        for plane in range(-LEFT, TILE):
            source = plane + 2
            value = zero
            if source < PLANES:
                value = smooth_rows(level[source * NY : (source + 1) * NY])
            for k in range(4):
                following = value + held[k]
                held[k] = value
                value = following
            if 0 <= plane < RIGHT:
                rim_ref[c, plane] = value
            elif plane >= TILE - LEFT:
                rim_ref[c, RIGHT + plane - (TILE - LEFT)] = value
            elif plane >= 0:
                inside_ref[c, plane - RIGHT] = value
        inside(c).start()
    for c in range(4):
        inside(c).wait()


def fine(spread, matrices):
    f32 = jnp.float32
    vmem = pl.BlockSpec(memory_space=pltpu.VMEM)
    return pl.pallas_call(
        fine_kernel,
        out_shape=[
            jax.ShapeDtypeStruct((4, TILE, NY, NZ), f32),
            jax.ShapeDtypeStruct((4, RIGHT + LEFT, NY, NZ), f32),
        ],
        in_specs=[vmem, pl.BlockSpec(memory_space=pltpu.HBM)],
        out_specs=[pl.BlockSpec(memory_space=pl.ANY), vmem],
        scratch_shapes=[
            pltpu.VMEM((4, TILE - RIGHT - LEFT, NY, NZ), f32),
            pltpu.VMEM((DEPTH_ROWS, 2 * NZ), jnp.bfloat16),
            pltpu.SemaphoreType.DMA((5,)),
        ],
        compiler_params=pltpu.CompilerParams(vmem_limit_bytes=44 * 2**20),
        cost_estimate=pl.CostEstimate(
            flops=4 * 2 * ROWS * 2 * NZ * NZ, bytes_accessed=10**7, transcendentals=0
        ),
        name="fine",
    )(spread, matrices)


def edge_rows(planes):
    return 4 * planes * (2 * NY + NY // 2 + NY // 4)


def deposit(arrived, matrices, per_peer, capacity):
    devices = arrived.shape[0]
    f32 = jnp.float32
    vmem = pl.BlockSpec(memory_space=pltpu.VMEM)
    return pl.pallas_call(
        functools.partial(deposit_kernel, per_peer, capacity // LANES),
        out_shape=[
            jax.ShapeDtypeStruct((4, ROWS, 2 * NZ), jnp.bfloat16),
            jax.ShapeDtypeStruct((4, NY // 2 * (TILE // 2), LANES), f32),
            jax.ShapeDtypeStruct((4, NY // 4 * (TILE // 4), LANES), f32),
            jax.ShapeDtypeStruct((edge_rows(RIGHT), LANES), f32),
            jax.ShapeDtypeStruct((edge_rows(LEFT), LANES), f32),
        ],
        in_specs=[vmem, pl.BlockSpec(memory_space=pltpu.HBM)],
        out_specs=[vmem] * 5,
        scratch_shapes=[
            pltpu.SMEM((NY // TILE * (NZ // TILE) + 1,), jnp.int32),
            pltpu.SMEM((devices, 1, per_peer * LANES), f32),
            pltpu.VMEM((TILE_ROWS, QUAD * capacity), jnp.bfloat16),
            pltpu.VMEM((TILE_ROWS, QUAD * capacity), jnp.bfloat16),
            pltpu.VMEM((WIDTH, QUAD * capacity), jnp.bfloat16),
            pltpu.VMEM((WIDTH, QUAD * capacity), jnp.bfloat16),
            pltpu.VMEM((QUADS, 2, NY // TILE, TILE_ROWS, WIDTH), f32),
            pltpu.VMEM((4, 2, 2 * NZ, 2 * LANES), jnp.bfloat16),
            pltpu.VMEM((4, 3 * (ROWS - 2 * NZ), 2 * LANES), jnp.bfloat16),
            pltpu.VMEM((DEPTH_ROWS + 3 * PLANE_ROWS, 2 * NZ), jnp.bfloat16),
            pltpu.SemaphoreType.DMA((2,)),
        ],
        compiler_params=pltpu.CompilerParams(vmem_limit_bytes=44 * 2**20),
        name="deposit",
    )(arrived, matrices)


def join_kernel(
    inside_ref, rim_ref, mid_in_ref, coarse_in_ref, low_ref, high_ref,
    fine_ref, mid_ref, coarse_ref, edge_ref, mid_sum, coarse_sum, sems,
):
    for c in range(4):
        for plane in range(RIGHT):
            row = (c * RIGHT + plane) * 2 * NY
            edge_ref[c, plane, :, :LANES] = rim_ref[c, plane, :, :LANES] + low_ref[row : row + NY]
            edge_ref[c, plane, :, LANES:] = (
                rim_ref[c, plane, :, LANES:] + low_ref[row + NY : row + 2 * NY]
            )
        for plane in range(LEFT):
            row = (c * LEFT + plane) * 2 * NY
            at = RIGHT + plane
            edge_ref[c, at, :, :LANES] = rim_ref[c, at, :, :LANES] + high_ref[row : row + NY]
            edge_ref[c, at, :, LANES:] = (
                rim_ref[c, at, :, LANES:] + high_ref[row + NY : row + 2 * NY]
            )
    first = pltpu.make_async_copy(edge_ref.at[:, :RIGHT], fine_ref.at[:, :RIGHT], sems.at[1])
    last = pltpu.make_async_copy(edge_ref.at[:, RIGHT:], fine_ref.at[:, TILE - LEFT :], sems.at[0])
    first.start()
    last.start()
    mid_sum[...] = mid_in_ref[...]
    coarse_sum[...] = coarse_in_ref[...]
    for sent, planes, first_of in ((low_ref, RIGHT, False), (high_ref, LEFT, True)):
        for c in range(4):
            for i in range(planes):
                count, edge = TILE // 2, NY // 2
                m = count - planes + i if first_of else i
                row = 4 * planes * 2 * NY + (c * planes + i) * edge
                where = pl.ds(m, edge, stride=count)
                mid_sum[c, where, :] = mid_sum[c, where, :] + sent[row : row + edge]
                count, edge = TILE // 4, NY // 4
                k = count - planes + i if first_of else i
                row = 4 * planes * (2 * NY + NY // 2) + (c * planes + i) * edge
                where = pl.ds(k, edge, stride=count)
                coarse_sum[c, where, :] = coarse_sum[c, where, :] + sent[row : row + edge]
    for c in range(4):
        for y in range(NY // 2):
            rows = TILE // 2
            mid_ref[c, :, y * LANES : (y + 1) * LANES] = mid_sum[c, y * rows : (y + 1) * rows]
        for pair in range(NY // 8):
            rows = TILE // 4
            even = coarse_sum[c, pair * rows : (pair + 1) * rows]
            at = NY // 8 * rows + pair * rows
            odd = coarse_sum[c, at : at + rows]
            lane = lax.broadcasted_iota(jnp.int32, even.shape, 1)
            coarse_ref[c, :, pair * LANES : (pair + 1) * LANES] = jnp.where(
                lane < LANES // 2, even, odd
            )
    first.wait()
    last.wait()


def join(inside, rim, mid, coarse, from_low, from_high):
    f32 = jnp.float32
    vmem = pl.BlockSpec(memory_space=pltpu.VMEM)
    far = pl.BlockSpec(memory_space=pl.ANY)
    return pl.pallas_call(
        join_kernel,
        out_shape=[
            jax.ShapeDtypeStruct((4, TILE, NY, NZ), f32),
            jax.ShapeDtypeStruct((4, TILE // 2, NY // 2 * (NZ // 2)), f32),
            jax.ShapeDtypeStruct((4, TILE // 4, NY // 4 * (NZ // 4)), f32),
        ],
        in_specs=[far] + [vmem] * 5,
        out_specs=[far, vmem, vmem],
        scratch_shapes=[
            pltpu.VMEM((4, RIGHT + LEFT, NY, NZ), f32),
            pltpu.VMEM(mid.shape, f32),
            pltpu.VMEM(coarse.shape, f32),
            pltpu.SemaphoreType.DMA((2,)),
        ],
        input_output_aliases={0: 0},
        compiler_params=pltpu.CompilerParams(vmem_limit_bytes=10 * 2**20),
        name="join",
    )(inside, rim, mid, coarse, from_low, from_high)


def on_device(positions, velocity, counts, tile_ids):
    held = positions.shape[0]
    capacity = positions.shape[2]
    devices = lax.axis_size("gx")
    per_peer = max(1, held // devices)
    matrices = jnp.asarray(filters())
    outgoing = bucket(positions, velocity, counts, tile_ids, devices, per_peer)
    arrived = lax.all_to_all(outgoing, "gx", split_axis=0, concat_axis=0, tiled=True)
    spread, mid, coarse, right, left = deposit(arrived, matrices, per_peer, capacity)
    from_low = lax.ppermute(right, "gx", [(i, (i + 1) % devices) for i in range(devices)])
    from_high = lax.ppermute(left, "gx", [(i, (i - 1) % devices) for i in range(devices)])
    inside, rim = fine(spread, matrices)
    return tuple(join(inside, rim, mid, coarse, from_low, from_high))


def solution(mesh):
    placed = (
        P(("snap", "gx"), None, None),
        P(("snap", "gx"), None, None),
        P(("snap", "gx")),
        P(("snap", "gx")),
    )
    return jax.shard_map(
        on_device,
        mesh=mesh,
        in_specs=placed,
        out_specs=(
            P(None, ("snap", "gx"), None, None),
            P(None, ("snap", "gx"), None),
            P(None, ("snap", "gx"), None),
        ),
        check_vma=False,
    )
```

```python
import functools
import math

import jax
import jax.numpy as jnp
import ml_dtypes
import numpy as np
from jax import lax
from jax.experimental import pallas as pl
from jax.experimental.pallas import tpu as pltpu
from jax.sharding import PartitionSpec as P

TILE = 16
NY = 32
NZ = 256
LANES = 128
QUAD = 4
PLANES = TILE + 1
ROWS = PLANES * NY
WIDTH = 4 * QUAD * TILE
QUADS = NZ // (QUAD * TILE)
MASS_UNIT = 4.0
DEAD = -32.0
BELOW = 32
TILE_ROWS = PLANES * TILE + BELOW
PLANE_ROWS = 288
DEPTH_ROWS = 4 * NZ
FILTER_ROWS = 18 * 1024

RIGHT = 3
LEFT = 2


def taps(levels):
    row = np.array([1.0])
    for level in range(levels):
        once = np.array([1.0, 4.0, 6.0, 4.0, 1.0]) / 16.0
        spread = np.zeros(4 * max(1, 2 ** (level - 1)) + 1)
        spread[:: max(1, 2 ** (level - 1))] = once
        row = np.convolve(row, spread)
    return row


def periodic(levels, size):
    step = 2 ** (levels - 1)
    row = taps(levels)
    half = len(row) // 2
    out = np.zeros((size // step, size))
    for i in range(size // step):
        for k, value in enumerate(row):
            out[i, (i * step + k - half) % size] += value
    return out


def open_ended(levels, below, above):
    step = 2 ** (levels - 1)
    row = taps(levels)
    half = len(row) // 2
    count = TILE // step
    out = np.zeros((below + count + above, PLANES))
    for i in range(-below, count + above):
        for k, value in enumerate(row):
            plane = i * step + k - half
            if 0 <= plane < PLANES:
                out[i + below, plane] += value
    return out


def split_host(matrix):
    high = matrix.astype(ml_dtypes.bfloat16)
    low = (matrix - high.astype(np.float64)).astype(ml_dtypes.bfloat16)
    return high, low


def depth_matrix():
    fine = periodic(1, NZ).T / 256.0
    mid = periodic(2, NZ).T
    coarse_high, coarse_low = split_host(periodic(3, NZ).T)
    columns = np.concatenate(
        [
            fine,
            mid,
            coarse_high.astype(np.float64),
            coarse_low.astype(np.float64),
        ],
        axis=1,
    )
    swapped = columns[np.arange(NZ) ^ (QUAD * TILE)]
    return np.concatenate([columns, columns, swapped, swapped]).astype(ml_dtypes.bfloat16)


def plane_matrix():
    mid_y = periodic(2, NY)
    coarse_y = periodic(3, NY)
    mid_x = open_ended(2, LEFT, RIGHT)
    coarse_x = open_ended(3, LEFT, RIGHT)
    rows = []
    for y in range(NY // 2):
        for m in range(TILE // 2):
            rows.append(np.kron(mid_x[LEFT + m], mid_y[y]))
    for m in list(range(-LEFT, 0)) + list(range(TILE // 2, TILE // 2 + RIGHT)):
        for y in range(NY // 2):
            rows.append(np.kron(mid_x[LEFT + m], mid_y[y]))
    order = list(range(0, NY // 4, 2)) + list(range(1, NY // 4, 2))
    for y in order:
        for k in range(TILE // 4):
            rows.append(np.kron(coarse_x[LEFT + k], coarse_y[y]))
    for k in list(range(-LEFT, 0)) + list(range(TILE // 4, TILE // 4 + RIGHT)):
        for y in order:
            rows.append(np.kron(coarse_x[LEFT + k], coarse_y[y]))
    rows += [np.zeros(ROWS)] * (PLANE_ROWS - len(rows))
    high, low = split_host(np.stack(rows))
    width = 2 * NZ
    ends = np.zeros((PLANE_ROWS, width), ml_dtypes.bfloat16)
    rest = ROWS - width
    for i, part in enumerate((high, high, low)):
        ends[:, i * rest : (i + 1) * rest] = part[:, width:]
    return np.concatenate([high[:, :width], low[:, :width], ends])


def filters():
    used = np.concatenate([depth_matrix(), plane_matrix()])
    return np.concatenate([used, np.zeros((FILTER_ROWS - len(used), used.shape[1]), used.dtype)])


def split(value):
    high = value.astype(jnp.bfloat16)
    return high, (value - high.astype(jnp.float32)).astype(jnp.bfloat16)


def depth_of(c):
    return slice(c % 2 * 2 * NZ, (c % 2 + 1) * 2 * NZ)


def smooth_rows(value):
    for _ in range(2):
        either = pltpu.roll(value, 1, 0) + pltpu.roll(value, value.shape[0] - 1, 0)
        value = either + 2.0 * value
    return value


def along_planes(fields, plane):
    total = None
    for shift, tap in zip(range(-2, 3), (1.0, 4.0, 6.0, 4.0, 1.0)):
        if plane + shift in fields:
            term = fields[plane + shift] if tap == 1.0 else tap * fields[plane + shift]
            total = term if total is None else total + term
    return total


def hat(position, lattice):
    return jnp.maximum(1.0 - jnp.abs(position - lattice), 0.0)


def bucket_kernel(
    per_peer, ids_far, counts_far, spots_far, speed_far, out_ref,
    filled_ref, ids_ref, counts_ref, spots_ref, speed_ref, sems,
):
    copies = [
        pltpu.make_async_copy(source, target, sems.at[i])
        for i, (source, target) in enumerate(
            (
                (ids_far, ids_ref),
                (counts_far, counts_ref),
                (spots_far, spots_ref),
                (speed_far, speed_ref),
            )
        )
    ]
    for copy in copies:
        copy.start()
    _, held, capacity = spots_ref.shape
    devices = out_ref.shape[0]
    size = 6 * capacity
    for owner in range(devices):
        filled_ref[owner] = 0
    for copy in copies:
        copy.wait()
    if devices * per_peer > held:
        marks = (devices, 1, per_peer * LANES)
        out_ref[:, :, per_peer * size :] = jnp.full(marks, -1.0, jnp.float32)

    for tile in range(held):
        tag = ids_ref[tile]
        count = counts_ref[tile]
        owner = tag // held
        rank = filled_ref[owner]
        filled_ref[owner] = rank + 1
        base = rank * size
        alive = lax.broadcasted_iota(jnp.int32, (1, capacity), 1) < count
        for a in range(6):
            source = spots_ref if a < 3 else speed_ref
            row = source[a % 3, tile : tile + 1, :]
            if a == 0:
                row = jnp.where(alive, row, DEAD)
            at = pl.multiple_of(base + a * capacity, LANES)
            out_ref[owner, :, pl.ds(at, capacity)] = row
        mark = jnp.full((1, LANES), (tag % held).astype(jnp.float32), jnp.float32)
        at = pl.multiple_of(per_peer * size + rank * LANES, LANES)
        out_ref[owner, :, pl.ds(at, LANES)] = mark


def bucket(positions, velocity, counts, tile_ids, devices, per_peer):
    capacity = positions.shape[2]
    columns = per_peer * (6 * capacity + LANES)
    return pl.pallas_call(
        functools.partial(bucket_kernel, per_peer),
        out_shape=jax.ShapeDtypeStruct((devices, 1, columns), jnp.float32),
        in_specs=[pl.BlockSpec(memory_space=pltpu.HBM)] * 4,
        out_specs=pl.BlockSpec(memory_space=pltpu.VMEM),
        scratch_shapes=[
            pltpu.SMEM((devices,), jnp.int32),
            pltpu.SMEM(tile_ids.shape, jnp.int32),
            pltpu.SMEM(counts.shape, jnp.int32),
            pltpu.VMEM((3,) + positions.shape[::2], jnp.float32),
            pltpu.VMEM((3,) + positions.shape[::2], jnp.float32),
            pltpu.SemaphoreType.DMA((4,)),
        ],
        compiler_params=pltpu.CompilerParams(vmem_limit_bytes=60 * 2**20),
        name="bucket",
    )(tile_ids, counts, positions.transpose(1, 0, 2), velocity.transpose(1, 0, 2))


def deposit_kernel(
    per_peer,
    chunks,
    arrived_ref,
    filter_far,
    spread_ref,
    mid_ref,
    coarse_ref,
    right_ref,
    left_ref,
    slot_ref,
    marks_ref,
    planar_even,
    planar_odd,
    depth_even,
    depth_odd,
    sums_ref,
    rest_ref,
    tails_ref,
    filter_ref,
    sems,
):
    devices = arrived_ref.shape[0]
    capacity = chunks * LANES
    size = 6 * capacity
    marks = pltpu.make_async_copy(arrived_ref.at[:, :, per_peer * size :], marks_ref, sems.at[0])
    marks.start()
    fetch = pltpu.make_async_copy(
        filter_far.at[: DEPTH_ROWS + 3 * PLANE_ROWS], filter_ref, sems.at[1]
    )
    fetch.start()
    planars, depths = (planar_even, planar_odd), (depth_even, depth_odd)
    for ref in depths:
        ref[...] = jnp.zeros(ref.shape, jnp.bfloat16)
    marks.wait()

    tiles = NY // TILE * (NZ // TILE)

    def look(slot, carry):
        tag = marks_ref[slot // per_peer, 0, slot % per_peer * LANES].astype(jnp.int32)
        slot_ref[jnp.where(tag < 0, tiles, tag)] = slot
        return carry

    if devices * per_peer == tiles:
        for slot in range(tiles):
            look(slot, 0)
    else:
        lax.fori_loop(0, devices * per_peer, look, 0)

    def row_of(shape, dim):
        return lax.broadcasted_iota(jnp.int32, shape, dim)

    x_lattice = row_of((BELOW, LANES), 0).astype(jnp.float32)
    cell_lattice = row_of((TILE, LANES), 0).astype(jnp.float32)
    first_row = row_of((TILE, LANES), 0) == 0

    def tile_terms(q, t, ty, buffer):
        slot = slot_ref[ty * (NZ // TILE) + q * QUAD + t]
        device = slot // per_peer
        base = (slot % per_peer) * size
        for chunk in range(chunks):

            def particle(a, rows):
                at = pl.multiple_of(base + (a * capacity + chunk * LANES), LANES)
                line = arrived_ref[device, :, pl.ds(at, LANES)]
                return jnp.broadcast_to(line, (rows, LANES))

            cut = slice(t * capacity + chunk * LANES, t * capacity + (chunk + 1) * LANES)
            weights_x = hat(particle(0, BELOW), x_lattice)
            weights_y = hat(particle(1, TILE), cell_lattice)
            for x in range(PLANES):
                planar = jnp.broadcast_to(weights_x[x : x + 1], (TILE, LANES)) * weights_y
                planars[buffer][x * TILE : (x + 1) * TILE, cut] = planar.astype(jnp.bfloat16)
            below = weights_x * jnp.maximum(particle(1, BELOW) - (TILE - 1.0), 0.0)
            planars[buffer][PLANES * TILE :, cut] = below.astype(jnp.bfloat16)

            spot_z = particle(2, TILE)
            weights_z = hat(spot_z, cell_lattice)
            past = jnp.where(first_row, jnp.maximum(spot_z - (TILE - 1.0), 0.0), 0.0)
            for c in range(4):
                charge = MASS_UNIT if c == 0 else MASS_UNIT * particle(2 + c, TILE)
                place = c ^ (q % 2)
                at = (place * QUAD + t) * TILE
                depths[buffer][at : at + TILE, cut] = (charge * weights_z).astype(
                    jnp.bfloat16
                )
                if t == QUAD - 1:
                    at = (place ^ 1) * QUAD * TILE
                else:
                    at = at + TILE
                depths[buffer][at : at + TILE, cut] = (charge * past).astype(jnp.bfloat16)

    def tile_sums(q, ty, buffer):
        for kind, cut in enumerate(
            (slice(0, (QUAD - 1) * capacity), slice((QUAD - 1) * capacity, QUAD * capacity))
        ):
            sums_ref[q, kind, ty] = lax.dot_general(
                planars[buffer][:, cut],
                depths[buffer][:, cut],
                (((1,), (1,)), ((), ())),
                preferred_element_type=jnp.float32,
            )

    steps = [(q, ty) for q in range(QUADS) for ty in range(NY // TILE)]
    for i, (q, ty) in enumerate(steps):
        if i:
            tile_sums(*steps[i - 1], (i - 1) % 2)
        for t in range(QUAD):
            tile_terms(q, t, ty, i % 2)
    tile_sums(*steps[-1], (len(steps) - 1) % 2)

    def window(q, ty, half, rows):
        cut = slice(half * LANES, (half + 1) * LANES)
        inner = row_of((rows.stop - rows.start, LANES), 1) % (LANES // 2) != 0
        return sums_ref[q, 0, ty, rows, cut] + jnp.where(
            inner, sums_ref[q, 1, ty, rows, cut], sums_ref[(q - 1) % QUADS, 1, ty, rows, cut]
        )

    first_half = row_of((TILE, LANES), 1) < LANES // 2
    for half in range(2):
        for h in range(2):
            for ty in range(NY // TILE):
                under = slice(PLANES * TILE, PLANES * TILE + BELOW)
                past = [window(2 * h + i, 1 - ty, half, under) for i in range(2)]
                for plane in range(PLANES):
                    rows = slice(plane * TILE, (plane + 1) * TILE)
                    even, odd = (
                        window(2 * h + i, ty, half, rows)
                        + jnp.where(
                            first_row,
                            jnp.broadcast_to(past[i][plane : plane + 1], (TILE, LANES)),
                            0.0,
                        )
                        for i in range(2)
                    )
                    rows = slice(plane * NY + ty * TILE, plane * NY + (ty + 1) * TILE)
                    for parity in range(2):
                        one, two = (even, odd) if parity == 0 else (odd, even)
                        high, low = split(jnp.where(first_half, one, two))
                        at = h * LANES
                        spread_ref[2 * half + parity, rows, at : at + LANES] = high
                        at += NZ
                        spread_ref[2 * half + parity, rows, at : at + LANES] = low

    fetch.wait()
    edge_planes = list(range(LEFT)) + list(range(PLANES - RIGHT, PLANES))

    width = 2 * NZ
    tall = ROWS - width

    def channel(c):
        rest = jnp.dot(spread_ref[c], filter_ref[depth_of(c), NZ:], preferred_element_type=jnp.float32)
        coarse = rest[:, LANES:]
        coarse = coarse + pltpu.roll(coarse, LANES // 2, 1)
        mid_high, mid_low = split(rest[:, :LANES])
        coarse_high, coarse_low = split(coarse)
        for i, (mid, rough) in enumerate(((mid_high, coarse_high), (mid_low, coarse_low))):
            rest_ref[c, i, :, :LANES] = mid[:width]
            rest_ref[c, i, :, LANES:] = rough[:width]
        for i, (mid, rough) in enumerate(
            ((mid_high, coarse_high), (mid_low, coarse_low), (mid_high, coarse_high))
        ):
            rows = slice(i * tall, (i + 1) * tall)
            tails_ref[c, rows, :LANES] = mid[width:]
            tails_ref[c, rows, LANES:] = rough[width:]

        edges = jnp.dot(
            jnp.concatenate(
                [spread_ref[c, : LEFT * NY], spread_ref[c, (PLANES - RIGHT) * NY :]], axis=0
            ),
            filter_ref[depth_of(c), :NZ],
            preferred_element_type=jnp.float32,
        )
        fields = {
            plane: smooth_rows(edges[i * NY : (i + 1) * NY]) for i, plane in enumerate(edge_planes)
        }
        for ref, planes, first in ((left_ref, LEFT, -LEFT), (right_ref, RIGHT, TILE)):
            for i in range(planes):
                value = along_planes(fields, first + i)
                row = (c * planes + i) * 2 * NY
                ref[row : row + NY, :] = value[:, :LANES]
                ref[row + NY : row + 2 * NY, :] = value[:, LANES:]

    def planes(c):
        at = DEPTH_ROWS + 2 * PLANE_ROWS
        packed = jnp.dot(
            filter_ref[at : at + PLANE_ROWS, : 3 * tall],
            tails_ref[c],
            preferred_element_type=jnp.float32,
        )
        for part, source in ((0, 0), (0, 1), (1, 0)):
            at = DEPTH_ROWS + part * PLANE_ROWS
            packed = packed + jnp.dot(
                filter_ref[at : at + PLANE_ROWS, :],
                rest_ref[c, source],
                preferred_element_type=jnp.float32,
            )
        mid_rows = NY // 2 * (TILE // 2)
        mid_edge = NY // 2
        mid_ref[c] = packed[:mid_rows, :LANES]
        at = mid_rows
        row = 4 * LEFT * 2 * NY + c * LEFT * mid_edge
        left_ref[pl.ds(pl.multiple_of(row, 8), LEFT * mid_edge), :] = packed[
            at : at + LEFT * mid_edge, :LANES
        ]
        at += LEFT * mid_edge
        row = 4 * RIGHT * 2 * NY + c * RIGHT * mid_edge
        right_ref[pl.ds(pl.multiple_of(row, 8), RIGHT * mid_edge), :] = packed[
            at : at + RIGHT * mid_edge, :LANES
        ]
        at += RIGHT * mid_edge
        coarse_rows = NY // 4 * (TILE // 4)
        coarse_edge = NY // 4
        coarse_ref[c] = packed[at : at + coarse_rows, LANES:]
        at += coarse_rows
        row = 4 * LEFT * (2 * NY + mid_edge) + c * LEFT * coarse_edge
        left_ref[pl.ds(pl.multiple_of(row, 8), LEFT * coarse_edge), :] = packed[
            at : at + LEFT * coarse_edge, LANES:
        ]
        at += LEFT * coarse_edge
        row = 4 * RIGHT * (2 * NY + mid_edge) + c * RIGHT * coarse_edge
        right_ref[pl.ds(pl.multiple_of(row, 8), RIGHT * coarse_edge), :] = packed[
            at : at + RIGHT * coarse_edge, LANES:
        ]

    channel(0)
    for c in range(4):
        if c < 3:
            channel(c + 1)
        planes(c)


def fine_kernel(spread_ref, filter_far, fine_ref, rim_ref, inside_ref, filter_ref, sems):
    fetch = pltpu.make_async_copy(filter_far.at[:DEPTH_ROWS], filter_ref, sems.at[4])
    fetch.start()
    fetch.wait()

    def inside(c):
        return pltpu.make_async_copy(
            inside_ref.at[c], fine_ref.at[c, RIGHT : TILE - LEFT], sems.at[c]
        )

    for c in range(4):
        level = jnp.dot(spread_ref[c], filter_ref[depth_of(c), :NZ], preferred_element_type=jnp.float32)
        zero = jnp.zeros((NY, NZ), jnp.float32)
        held = [zero] * 4
        for plane in range(-LEFT, TILE):
            source = plane + 2
            value = zero
            if source < PLANES:
                value = smooth_rows(level[source * NY : (source + 1) * NY])
            for k in range(4):
                following = value + held[k]
                held[k] = value
                value = following
            if 0 <= plane < RIGHT:
                rim_ref[c, plane] = value
            elif plane >= TILE - LEFT:
                rim_ref[c, RIGHT + plane - (TILE - LEFT)] = value
            elif plane >= 0:
                inside_ref[c, plane - RIGHT] = value
        inside(c).start()
    for c in range(4):
        inside(c).wait()


def fine(spread, matrices):
    f32 = jnp.float32
    vmem = pl.BlockSpec(memory_space=pltpu.VMEM)
    return pl.pallas_call(
        fine_kernel,
        out_shape=[
            jax.ShapeDtypeStruct((4, TILE, NY, NZ), f32),
            jax.ShapeDtypeStruct((4, RIGHT + LEFT, NY, NZ), f32),
        ],
        in_specs=[vmem, pl.BlockSpec(memory_space=pltpu.HBM)],
        out_specs=[pl.BlockSpec(memory_space=pl.ANY), vmem],
        scratch_shapes=[
            pltpu.VMEM((4, TILE - RIGHT - LEFT, NY, NZ), f32),
            pltpu.VMEM((DEPTH_ROWS, 2 * NZ), jnp.bfloat16),
            pltpu.SemaphoreType.DMA((5,)),
        ],
        compiler_params=pltpu.CompilerParams(vmem_limit_bytes=44 * 2**20),
        cost_estimate=pl.CostEstimate(
            flops=4 * 2 * ROWS * 2 * NZ * NZ, bytes_accessed=10**7, transcendentals=0
        ),
        name="fine",
    )(spread, matrices)


def edge_rows(planes):
    return 4 * planes * (2 * NY + NY // 2 + NY // 4)


def deposit(arrived, matrices, per_peer, capacity):
    devices = arrived.shape[0]
    f32 = jnp.float32
    vmem = pl.BlockSpec(memory_space=pltpu.VMEM)
    return pl.pallas_call(
        functools.partial(deposit_kernel, per_peer, capacity // LANES),
        out_shape=[
            jax.ShapeDtypeStruct((4, ROWS, 2 * NZ), jnp.bfloat16),
            jax.ShapeDtypeStruct((4, NY // 2 * (TILE // 2), LANES), f32),
            jax.ShapeDtypeStruct((4, NY // 4 * (TILE // 4), LANES), f32),
            jax.ShapeDtypeStruct((edge_rows(RIGHT), LANES), f32),
            jax.ShapeDtypeStruct((edge_rows(LEFT), LANES), f32),
        ],
        in_specs=[vmem, pl.BlockSpec(memory_space=pltpu.HBM)],
        out_specs=[vmem] * 5,
        scratch_shapes=[
            pltpu.SMEM((NY // TILE * (NZ // TILE) + 1,), jnp.int32),
            pltpu.SMEM((devices, 1, per_peer * LANES), f32),
            pltpu.VMEM((TILE_ROWS, QUAD * capacity), jnp.bfloat16),
            pltpu.VMEM((TILE_ROWS, QUAD * capacity), jnp.bfloat16),
            pltpu.VMEM((WIDTH, QUAD * capacity), jnp.bfloat16),
            pltpu.VMEM((WIDTH, QUAD * capacity), jnp.bfloat16),
            pltpu.VMEM((QUADS, 2, NY // TILE, TILE_ROWS, WIDTH), f32),
            pltpu.VMEM((4, 2, 2 * NZ, 2 * LANES), jnp.bfloat16),
            pltpu.VMEM((4, 3 * (ROWS - 2 * NZ), 2 * LANES), jnp.bfloat16),
            pltpu.VMEM((DEPTH_ROWS + 3 * PLANE_ROWS, 2 * NZ), jnp.bfloat16),
            pltpu.SemaphoreType.DMA((2,)),
        ],
        compiler_params=pltpu.CompilerParams(vmem_limit_bytes=44 * 2**20),
        name="deposit",
    )(arrived, matrices)


def join_kernel(
    inside_ref, rim_ref, mid_in_ref, coarse_in_ref, low_ref, high_ref,
    fine_ref, mid_far, coarse_far, edge_ref, mid_ref, coarse_ref, mid_sum, coarse_sum, sems,
):
    mid_sum[...] = mid_in_ref[...]
    coarse_sum[...] = coarse_in_ref[...]
    for sent, planes, first_of in ((low_ref, RIGHT, False), (high_ref, LEFT, True)):
        for c in range(4):
            for i in range(planes):
                count, edge = TILE // 2, NY // 2
                m = count - planes + i if first_of else i
                row = 4 * planes * 2 * NY + (c * planes + i) * edge
                where = pl.ds(m, edge, stride=count)
                mid_sum[c, where, :] = mid_sum[c, where, :] + sent[row : row + edge]
                count, edge = TILE // 4, NY // 4
                k = count - planes + i if first_of else i
                row = 4 * planes * (2 * NY + NY // 2) + (c * planes + i) * edge
                where = pl.ds(k, edge, stride=count)
                coarse_sum[c, where, :] = coarse_sum[c, where, :] + sent[row : row + edge]
    for c in range(4):
        for y in range(NY // 2):
            rows = TILE // 2
            mid_ref[c, :, y * LANES : (y + 1) * LANES] = mid_sum[c, y * rows : (y + 1) * rows]
        for pair in range(NY // 8):
            rows = TILE // 4
            even = coarse_sum[c, pair * rows : (pair + 1) * rows]
            at = NY // 8 * rows + pair * rows
            odd = coarse_sum[c, at : at + rows]
            lane = lax.broadcasted_iota(jnp.int32, even.shape, 1)
            coarse_ref[c, :, pair * LANES : (pair + 1) * LANES] = jnp.where(
                lane < LANES // 2, even, odd
            )
    mid_out = pltpu.make_async_copy(mid_ref, mid_far, sems.at[2])
    coarse_out = pltpu.make_async_copy(coarse_ref, coarse_far, sems.at[3])
    mid_out.start()
    coarse_out.start()
    for c in range(4):
        for plane in range(RIGHT):
            row = (c * RIGHT + plane) * 2 * NY
            edge_ref[c, plane, :, :LANES] = rim_ref[c, plane, :, :LANES] + low_ref[row : row + NY]
            edge_ref[c, plane, :, LANES:] = (
                rim_ref[c, plane, :, LANES:] + low_ref[row + NY : row + 2 * NY]
            )
        for plane in range(LEFT):
            row = (c * LEFT + plane) * 2 * NY
            at = RIGHT + plane
            edge_ref[c, at, :, :LANES] = rim_ref[c, at, :, :LANES] + high_ref[row : row + NY]
            edge_ref[c, at, :, LANES:] = (
                rim_ref[c, at, :, LANES:] + high_ref[row + NY : row + 2 * NY]
            )
    first = pltpu.make_async_copy(edge_ref.at[:, :RIGHT], fine_ref.at[:, :RIGHT], sems.at[1])
    last = pltpu.make_async_copy(edge_ref.at[:, RIGHT:], fine_ref.at[:, TILE - LEFT :], sems.at[0])
    first.start()
    last.start()
    first.wait()
    last.wait()
    mid_out.wait()
    coarse_out.wait()


def join(inside, rim, mid, coarse, from_low, from_high):
    f32 = jnp.float32
    vmem = pl.BlockSpec(memory_space=pltpu.VMEM)
    far = pl.BlockSpec(memory_space=pl.ANY)
    return pl.pallas_call(
        join_kernel,
        out_shape=[
            jax.ShapeDtypeStruct((4, TILE, NY, NZ), f32),
            jax.ShapeDtypeStruct((4, TILE // 2, NY // 2 * (NZ // 2)), f32),
            jax.ShapeDtypeStruct((4, TILE // 4, NY // 4 * (NZ // 4)), f32),
        ],
        in_specs=[far] + [vmem] * 5,
        out_specs=[far] * 3,
        scratch_shapes=[
            pltpu.VMEM((4, RIGHT + LEFT, NY, NZ), f32),
            pltpu.VMEM((4, TILE // 2, NY // 2 * (NZ // 2)), f32),
            pltpu.VMEM((4, TILE // 4, NY // 4 * (NZ // 4)), f32),
            pltpu.VMEM(mid.shape, f32),
            pltpu.VMEM(coarse.shape, f32),
            pltpu.SemaphoreType.DMA((4,)),
        ],
        input_output_aliases={0: 0},
        compiler_params=pltpu.CompilerParams(vmem_limit_bytes=10 * 2**20),
        name="join",
    )(inside, rim, mid, coarse, from_low, from_high)


def on_device(positions, velocity, counts, tile_ids):
    held = positions.shape[0]
    capacity = positions.shape[2]
    devices = lax.axis_size("gx")
    per_peer = max(1, held // devices)
    matrices = jnp.asarray(filters())
    outgoing = bucket(positions, velocity, counts, tile_ids, devices, per_peer)
    arrived = lax.all_to_all(outgoing, "gx", split_axis=0, concat_axis=0, tiled=True)
    spread, mid, coarse, right, left = deposit(arrived, matrices, per_peer, capacity)
    from_low = lax.ppermute(right, "gx", [(i, (i + 1) % devices) for i in range(devices)])
    from_high = lax.ppermute(left, "gx", [(i, (i - 1) % devices) for i in range(devices)])
    inside, rim = fine(spread, matrices)
    return tuple(join(inside, rim, mid, coarse, from_low, from_high))


def solution(mesh):
    placed = (
        P(("snap", "gx"), None, None),
        P(("snap", "gx"), None, None),
        P(("snap", "gx")),
        P(("snap", "gx")),
    )
    return jax.shard_map(
        on_device,
        mesh=mesh,
        in_specs=placed,
        out_specs=(
            P(None, ("snap", "gx"), None, None),
            P(None, ("snap", "gx"), None),
            P(None, ("snap", "gx"), None),
        ),
        check_vma=False,
    )
```
